128 devices in a mesh: stn: 16 (over x, z_hi, core), chan: 8 (over z_lo, y).
Axes of the slice: x: 4, y: 4, z: 4 (z_hi: 2, z_lo: 2; z = z_hi * 2 + z_lo), core: 2. Of those that a mesh axis runs over, the one named last changes fastest.
Arguments:
- voltages: bfloat16 [256, 2, 512, 1024], P('stn', None, 'chan'), may hold values from -6 to 6
- taps: float32 [4, 512], replicated, may hold values from 0.25 to 1
- flags: int32 [256], P('stn'), may hold values 0 or 1
Outputs:
- stokes: float32 [512, 8, 256, 256], P('chan', None, 'stn')
The draws below stay inside these ranges and needn't reach their ends.
Inputs may be any that keep to these rules, and one draw needn't show every extreme that they name: 1 keeps a station, 0 flags it.
All inputs are finite; a program needn't handle non-finite values. No bound on the sum of `flags` on one device may be relied on, other than what follows from the above.
Results may differ from the reference program's by a relative error of at most 0.0048.
Values may be sent and summed in bfloat16 or wider, within the bound.
A program may use at most 128 MiB of HBM per device.

```python
import math
import jax
import jax.numpy as jnp
from jax import lax

STATIONS = 256
CHANNELS = 512
TAPS = 4
NSPEC = 512


def place_ends(entries, own_key, smallest, high):
    spot = [jax.random.randint(jax.random.fold_in(own_key, axis), (), 0, length) for axis, length in enumerate(entries.shape)]
    widest = entries.shape.index(max(entries.shape))
    beside = spot[:widest] + [(spot[widest] + 1) % entries.shape[widest]] + spot[widest + 1:]
    return entries.at[tuple(spot)].set(smallest).at[tuple(beside)].set(high)


def level_of(key, dims, shards, smallest, top_value):
    def one(position, parts):
        steps = jax.random.uniform(jax.random.fold_in(jax.random.fold_in(key, 6), position), (parts,), jnp.float32, smallest / len(shards), top_value / len(shards))
        return jnp.repeat(jnp.exp(steps), dims[position] // parts).reshape((-1,) + (1,) * (len(dims) - position - 1))

    factor_of = one(*shards[0])
    for cut in shards[1:]:
        factor_of = factor_of * one(*cut)
    return factor_of


def bell_draw(rng, dims, deviation, reach, split=(), kind=jnp.bfloat16):
    drawn = deviation * jax.random.normal(rng, dims, jnp.float32)
    if split:
        drawn = drawn * level_of(rng, dims, split, -0.22, 0.18)
    return jnp.clip(drawn, -reach, reach).astype(kind)


def setup_inputs(seed: int = 0) -> dict:
    streams_of = jax.random.split(jax.random.key(seed), 4)
    voltages = bell_draw(streams_of[0], (STATIONS, 2, NSPEC, 2 * CHANNELS), 1.0, 6.0, ((0, 16), (2, 8)))
    taps = jnp.clip(jax.random.uniform(streams_of[1], (TAPS, CHANNELS), jnp.float32, 0.25, 1.0), 0.25, 1.0)
    flags = place_ends((jax.random.randint(streams_of[2], (STATIONS,), 0, 8) < 7).astype(jnp.int32), jax.random.fold_in(streams_of[2], 1), 0, 1)
    return {"voltages": voltages, "taps": taps, "flags": flags}


def dft_table(columns):
    channel_count = columns.shape[0]
    samples = jnp.arange(channel_count, dtype=jnp.int32)
    product = samples[:, None] * columns[None, :] % channel_count
    angles = 2.0 * math.pi / channel_count * product.astype(jnp.float32)
    factor = 1.0 / math.sqrt(channel_count)
    cosine = jnp.cos(angles) * factor
    sine_part = jnp.sin(angles) * factor
    upper_half = jnp.concatenate([cosine, -sine_part], axis=1)
    lower_half = jnp.concatenate([sine_part, cosine], axis=1)
    return jnp.concatenate([upper_half, lower_half], axis=0).astype(jnp.bfloat16)

def stokes_terms(gram_matrix, factor):
    real_real = gram_matrix[:, :, 0, :, :, 0]
    imag_imag = gram_matrix[:, :, 1, :, :, 1]
    imag_real = gram_matrix[:, :, 1, :, :, 0]
    real_imag = gram_matrix[:, :, 0, :, :, 1]
    corr_real = (real_real + imag_imag) * factor
    corr_imag = (imag_real - real_imag) * factor
    xx_real = corr_real[:, 0, :, 0]
    xx_imag = corr_imag[:, 0, :, 0]
    yy_real = corr_real[:, 1, :, 1]
    yy_imag = corr_imag[:, 1, :, 1]
    xy_real = corr_real[:, 0, :, 1]
    xy_imag = corr_imag[:, 0, :, 1]
    yx_real = corr_real[:, 1, :, 0]
    yx_imag = corr_imag[:, 1, :, 0]
    return jnp.stack([xx_real + yy_real, xx_imag + yy_imag, xx_real - yy_real, xx_imag - yy_imag, xy_real + yx_real, xy_imag + yx_imag, xy_imag - yx_imag, yx_real - xy_real], axis=0)

def reference(voltages, taps, flags):
    transform = dft_table(jnp.arange(CHANNELS, dtype=jnp.int32)).astype(jnp.float32)
    taps_both = jnp.concatenate([taps, taps], axis=1).astype(jnp.float32)

    def one_station(inputs):
        samples, weight = inputs
        padded = jnp.concatenate([jnp.zeros((2, TAPS - 1, 2 * CHANNELS), samples.dtype), samples], axis=1).astype(jnp.float32)
        filtered = jnp.zeros((2, NSPEC, 2 * CHANNELS), jnp.float32)
        for offset in range(TAPS):
            filtered = filtered + taps_both[offset] * padded[:, offset:offset + NSPEC, :]
        filtered = filtered.astype(jnp.bfloat16).astype(jnp.float32)
        spectra = jnp.dot(filtered.reshape(-1, 2 * CHANNELS), transform, precision=lax.Precision.HIGHEST)
        spectra = spectra.astype(jnp.bfloat16) * weight.astype(jnp.bfloat16)
        return spectra.reshape(2, NSPEC, 2 * CHANNELS)
    spectra = lax.map(one_station, (voltages, flags))
    by_channel = jnp.transpose(spectra.reshape(STATIONS, 2, NSPEC, 2, CHANNELS), (4, 0, 1, 2, 3))

    def one_channel(channel_block):
        block_wide = channel_block.astype(jnp.float32)
        gram_matrix = lax.dot_general(block_wide, block_wide, (((2,), (2,)), ((), ())), precision=lax.Precision.HIGHEST)
        return stokes_terms(gram_matrix, 1.0 / NSPEC)
    return lax.map(one_channel, by_channel)
```

```python
import functools
import math

import jax
import jax.numpy as jnp
import numpy as np
from jax import lax
from jax.experimental import pallas as pl
from jax.experimental.pallas import tpu as pltpu
from jax.sharding import PartitionSpec as P

CHANNELS = 512
TAPS = 4
LANES = 128
MESH = pl.DeviceIdType.MESH


def half_table(stn_count, chan_count):
    per_device = CHANNELS // (stn_count * chan_count)
    stn, chan, own = np.meshgrid(
        np.arange(stn_count), np.arange(chan_count), np.arange(per_device), indexing="ij"
    )
    rows = jnp.asarray((chan * stn_count * per_device + stn * per_device + own).reshape(-1), jnp.int32)
    samples = jnp.arange(CHANNELS, dtype=jnp.int32)
    angles = 2.0 * math.pi / CHANNELS * (rows[:, None] * samples[None, :] % CHANNELS).astype(jnp.float32)
    factor = 1.0 / math.sqrt(CHANNELS)
    table = jnp.concatenate([jnp.cos(angles) * factor, jnp.sin(angles) * factor], axis=1)
    return table.astype(jnp.bfloat16)


def kernel(
    volt_hbm, taps_ref, flags_ref, table_hbm, out_ref,
    volt, table, raw, mixed, planes, a_src, a_dst, terms, b_src, halo_src, halo_dst,
    load_sem, halo_sem, a_send, a_recv, b_send, b_recv,
):
    stn_count, chan_count = lax.axis_size("stn"), lax.axis_size("chan")
    count = stn_count * chan_count
    stn, chan = lax.axis_index("stn"), lax.axis_index("chan")
    me = stn * chan_count + chan
    feeds, steps = volt.shape[0], volt.shape[1]
    stations = feeds // 2
    pitch = steps + 8
    per_device = CHANNELS // count
    parts = load_sem.shape[0] - 1
    share = feeds // parts

    def owner(index):
        return (index // chan_count, index % chan_count)

    def partner(step):
        return (me + step) % count

    table_copy = pltpu.make_async_copy(table_hbm, table, load_sem.at[parts])
    for part in range(parts):
        span = pl.ds(part * share, share)
        pltpu.make_async_copy(volt_hbm.at[span], volt.at[span], load_sem.at[part]).start()
    table_copy.start()

    barrier = pltpu.get_barrier_semaphore()

    @pl.loop(1, count)
    def _(step):
        pl.semaphore_signal(barrier, inc=1, device_id=owner(partner(step)), device_id_type=MESH)

    for part in range(parts):
        span = pl.ds(part * share, share)
        pltpu.make_async_copy(volt_hbm.at[span], volt.at[span], load_sem.at[part]).wait()

        @pl.loop(part * share, (part + 1) * share)
        def _(feed):
            flag = flags_ref[feed // 2].astype(jnp.float32)
            for tile in range(8):
                block = volt[feed, :, tile * LANES : (tile + 1) * LANES].astype(jnp.float32) * flag
                raw[tile, pl.ds(pl.multiple_of(feed * pitch + 8, 8), steps), :] = block

    for tile in range(8):
        for back in range(TAPS - 1):
            rows = raw[tile, pl.ds(8 + steps - (TAPS - 1) + back, feeds, stride=pitch), :]
            halo_src[pl.ds(back * feeds, feeds), pl.ds(tile * LANES, LANES)] = rows.astype(jnp.bfloat16)

    def filtered(first):
        @pl.loop(0, feeds)
        def _(feed):
            station, polar = feed // 2, feed % 2
            for tile in range(8):
                weights = [
                    taps_ref[pl.ds(tap, 1), pl.ds((tile % 4) * LANES, LANES)] for tap in range(TAPS)
                ]
                rows = [
                    raw[tile, pl.ds(feed * pitch + 8 + first - 3 + shift, 8, stride=8), :]
                    for shift in range(7)
                ]
                sums = []
                for index in range(4):
                    total = weights[0] * rows[index]
                    for tap in range(1, TAPS):
                        total = total + weights[tap] * rows[index + tap]
                    sums.append(total)
                block = jnp.concatenate(sums, axis=0).astype(jnp.bfloat16)
                base = station * LANES + polar * 32
                mixed[pl.ds(pl.multiple_of(base, 32), 32), tile * LANES : (tile + 1) * LANES] = block
                other = (tile + 4) % 8
                turned = block if tile >= 4 else -block
                mixed[
                    pl.ds(pl.multiple_of(base + 64, 32), 32), other * LANES : (other + 1) * LANES
                ] = turned

    def transformed(half):
        @pl.loop(0, stations // 2)
        def _(pair):
            rows = mixed[pl.ds(pl.multiple_of(pair * 256, 256), 256), :]
            out = lax.dot_general(
                table[...], rows, (((1,), (1,)), ((), ())), preferred_element_type=jnp.float32
            )
            planes[pl.ds(2 * pair, CHANNELS, stride=stations), :] = out[:, :LANES]
            planes[pl.ds(2 * pair + 1, CHANNELS, stride=stations), :] = out[:, LANES:]

        depth = per_device * stations
        group = 8

        @pl.loop(0, count // group)
        def _(block):
            rows = planes[pl.ds(pl.multiple_of(block * (group * depth), group * depth), group * depth), :]
            a_src[half, pl.ds(block * group, group)] = rows.astype(jnp.bfloat16).reshape(group, depth, LANES)

    filtered(4)
    table_copy.wait()
    transformed(0)
    pl.semaphore_wait(barrier, count - 1)

    after = (stn, (chan + 1) % chan_count)
    halo_copy = pltpu.make_async_remote_copy(
        src_ref=halo_src, dst_ref=halo_dst, send_sem=halo_sem.at[0], recv_sem=halo_sem.at[1],
        device_id=after, device_id_type=MESH,
    )
    halo_copy.start()

    def a_copy(half, span, slot, index):
        return pltpu.make_async_remote_copy(
            src_ref=a_src.at[half, index, span], dst_ref=a_dst.at[half, me, span],
            send_sem=a_send.at[slot], recv_sem=a_recv.at[slot],
            device_id=owner(index), device_id_type=MESH,
        )

    def a_all(half, span, slot):
        ref = a_dst.at[half, pl.ds(0, count - 1), span]
        return pltpu.make_async_remote_copy(
            src_ref=ref, dst_ref=ref, send_sem=a_send.at[slot], recv_sem=a_recv.at[slot],
            device_id=owner(me), device_id_type=MESH,
        )

    whole = pl.ds(0, per_device * stations)
    halves = [pl.ds(part * 2 * stations, 2 * stations) for part in range(per_device // 2)]

    @pl.loop(1, count)
    def _(step):
        a_copy(0, whole, 0, partner(step)).start()

    a_dst[0, me] = a_src[0, me]

    halo_copy.wait()
    for tile in range(8):
        for back in range(TAPS - 1):
            rows = halo_dst[pl.ds(back * feeds, feeds), pl.ds(tile * LANES, LANES)].astype(jnp.float32)
            rows = jnp.where(chan == 0, 0.0, rows)
            raw[tile, pl.ds(8 - (TAPS - 1) + back, feeds, stride=pitch), :] = rows

    filtered(0)
    transformed(1)
    a_dst[1, me] = a_src[1, me]

    for part, span in enumerate(halves):
        @pl.loop(1, count)
        def _(step):
            a_copy(1, span, 1 + part, partner(step)).start()

    lane = lax.broadcasted_iota(jnp.int32, (1, LANES), 1)
    first_polar = lane % 64 < 32
    polar_sign = jnp.where(first_polar, 1.0, -1.0)
    turn_sign = jnp.where(lane < 64, 1.0, -1.0)
    rows_total = stn_count * stations

    def correlated(own):
        for half in range(2):
            @pl.loop(0, chan_count)
            def _(source):
                x = jnp.concatenate(
                    [
                        a_dst[half, block * chan_count + source, own * stations : (own + 1) * stations, :]
                        for block in range(stn_count)
                    ],
                    axis=0,
                ).astype(jnp.float32)
                swapped = jnp.where(first_polar, pltpu.roll(x, 96, 1), pltpu.roll(x, 32, 1))
                turned = pltpu.roll(x, 64, 1) * turn_sign
                both = pltpu.roll(swapped, 64, 1) * turn_sign
                values = [
                    x, turned, x * polar_sign, turned * polar_sign,
                    swapped, both, both * -polar_sign, swapped * polar_sign,
                ]
                lanes = pl.ds(pl.multiple_of((half * chan_count + source) * LANES, LANES), LANES)
                for index, value in enumerate(values):
                    terms[index * rows_total : (index + 1) * rows_total, lanes] = value.astype(jnp.bfloat16)

        @pl.loop(0, 4)
        def _(quarter):
            left = terms[pl.ds(pl.multiple_of(quarter * 2 * rows_total, 2 * rows_total), 2 * rows_total), :]
            out = lax.dot_general(
                left, terms[:rows_total, :], (((1,), (1,)), ((), ())), preferred_element_type=jnp.float32
            ).astype(jnp.bfloat16)
            for which in range(2):
                rows = out[which * rows_total : (which + 1) * rows_total]
                b_src[own, :, 2 * quarter + which] = rows.reshape(stn_count, stations, rows_total)

    for own in range(per_device):
        if own == 0:
            a_all(0, whole, 0).wait()
        if own % 2 == 0:
            a_all(1, halves[own // 2], 1 + own // 2).wait()
        correlated(own)

        @pl.loop(1, stn_count)
        def _(step):
            target = (stn + step) % stn_count
            pltpu.make_async_remote_copy(
                src_ref=b_src.at[own, target], dst_ref=out_ref.at[stn * per_device + own],
                send_sem=b_send, recv_sem=b_recv, device_id=(target, chan), device_id_type=MESH,
            ).start()

        out_ref[stn * per_device + own] = b_src[own, stn]

    ref = out_ref.at[pl.ds(0, (stn_count - 1) * per_device)]
    pltpu.make_async_remote_copy(
        src_ref=ref, dst_ref=ref, send_sem=b_send, recv_sem=b_recv,
        device_id=owner(me), device_id_type=MESH,
    ).wait()


def on_device(voltages, taps, flags):
    stn_count, chan_count = lax.axis_size("stn"), lax.axis_size("chan")
    count = stn_count * chan_count
    stations, polars, steps, width = voltages.shape
    feeds = stations * polars
    per_device = CHANNELS // count
    total = stn_count * stations
    vmem = pltpu.VMEM
    narrow = pl.pallas_call(
        kernel,
        out_shape=jax.ShapeDtypeStruct((CHANNELS // chan_count, 8, stations, total), jnp.bfloat16),
        in_specs=[
            pl.BlockSpec(memory_space=pl.ANY),
            pl.BlockSpec(memory_space=vmem),
            pl.BlockSpec(memory_space=pltpu.SMEM),
            pl.BlockSpec(memory_space=pl.ANY),
        ],
        out_specs=pl.BlockSpec(memory_space=vmem),
        scratch_shapes=[
            vmem((feeds, steps, width), jnp.bfloat16),
            vmem((CHANNELS, width), jnp.bfloat16),
            vmem((8, feeds * (steps + 8), LANES), jnp.float32),
            vmem((stations * LANES, width), jnp.bfloat16),
            vmem((CHANNELS * stations, LANES), jnp.float32),
            vmem((2, count, per_device * stations, LANES), jnp.bfloat16),
            vmem((2, count, per_device * stations, LANES), jnp.bfloat16),
            vmem((8 * total, 2 * chan_count * LANES), jnp.bfloat16),
            vmem((per_device, stn_count, 8, stations, total), jnp.bfloat16),
            vmem(((TAPS - 1) * feeds, width), jnp.bfloat16),
            vmem(((TAPS - 1) * feeds, width), jnp.bfloat16),
            pltpu.SemaphoreType.DMA((5,)),
            pltpu.SemaphoreType.DMA((2,)),
            pltpu.SemaphoreType.DMA((3,)),
            pltpu.SemaphoreType.DMA((3,)),
            pltpu.SemaphoreType.DMA,
            pltpu.SemaphoreType.DMA,
        ],
        compiler_params=pltpu.CompilerParams(
            collective_id=0, has_side_effects=True, vmem_limit_bytes=60 * 1024 * 1024
        ),
        name="correlate",
    )(voltages.reshape(feeds, steps, width), taps, flags, half_table(stn_count, chan_count))
    return narrow.astype(jnp.float32) * (1.0 / (steps * chan_count))


def solution(mesh):
    return jax.shard_map(
        on_device,
        mesh=mesh,
        in_specs=(P("stn", None, "chan", None), P(), P("stn")),
        out_specs=P("chan", None, "stn", None),
        check_vma=False,
    )
```

```python
import functools
import math

import jax
import jax.numpy as jnp
import numpy as np
from jax import lax
from jax.experimental import pallas as pl
from jax.experimental.pallas import tpu as pltpu
from jax.sharding import PartitionSpec as P

CHANNELS = 512
TAPS = 4
LANES = 128
MESH = pl.DeviceIdType.MESH


def half_table(stn_count, chan_count):
    per_device = CHANNELS // (stn_count * chan_count)
    pair, stn, chan, own = np.meshgrid(
        np.arange(per_device // 2), np.arange(stn_count), np.arange(chan_count), np.arange(2), indexing="ij"
    )
    rows = (chan * stn_count * per_device + stn * per_device + pair * 2 + own).reshape(-1)
    turns = (rows[:, None] * np.arange(CHANNELS)[None, :] % CHANNELS).astype(np.float32)
    angles = np.float32(2.0 * math.pi / CHANNELS) * turns
    factor = np.float32(1.0 / math.sqrt(CHANNELS))
    table = np.concatenate([np.cos(angles) * factor, np.sin(angles) * factor], axis=1)
    return jnp.asarray(table.astype(jnp.bfloat16))


def kernel(
    volt_hbm, taps_ref, flags_ref, table_hbm, out_ref,
    volt, table, raw, mixed, planes, a_src, a_dst, terms, b_src, halo_src, halo_dst,
    load_sem, halo_send, halo_recv, a_send, a_recv, b_send, b_recv, own_sem,
):
    stn_count, chan_count = lax.axis_size("stn"), lax.axis_size("chan")
    count = stn_count * chan_count
    stn, chan = lax.axis_index("stn"), lax.axis_index("chan")
    me = stn * chan_count + chan
    feeds, steps = volt.shape[0], volt.shape[1]
    stations = feeds // 2
    pitch = steps + 8
    per_device = CHANNELS // count
    parts = load_sem.shape[0] - 1
    share = feeds // parts

    def owner(index):
        return (index // chan_count, index % chan_count)

    x, z, core, y = stn // 4, (stn // 2 % 2) * 2 + chan // 4, stn % 2, chan % 4
    along_x = [(x + step) % 4 * 32 for step in range(4)]
    along_y = [(y + step) % 4 for step in range(4)]

    def plane_of(outer):
        other_z = (z + outer + 1) % 4
        return other_z // 2 * 16 + other_z % 2 * 4 + (core + outer // 4) % 2 * 8

    def each_partner(act):
        @pl.loop(0, 8)
        def _(outer):
            base = plane_of(outer)
            for step_y in range(4):
                for step_x in range(4):
                    index = base + along_x[step_x] + along_y[step_y]
                    if step_x == 0 and step_y == 0:
                        pl.when(outer != 3)(functools.partial(act, index))
                    else:
                        act(index)

    table_copy = pltpu.make_async_copy(table_hbm, table, load_sem.at[parts])
    loads = []
    for part in range(parts):
        span = pl.ds(part * share, share)
        loads.append(pltpu.make_async_copy(volt_hbm.at[span], volt.at[span], load_sem.at[part]))
        loads[-1].start()
    table_copy.start()

    barrier = pltpu.get_barrier_semaphore()

    def greet(index):
        pl.semaphore_signal(barrier, inc=1, device_id=owner(index), device_id_type=MESH)

    for part in range(parts):
        loads[part].wait()

        @pl.loop(part * share, (part + 1) * share)
        def _(feed):
            base = plane_of(feed // 4) + (y + feed % 4) % 4
            pl.when(feed != 12)(functools.partial(greet, base + along_x[0]))
            for step_x in range(1, 4):
                greet(base + along_x[step_x])
            flag = flags_ref[feed // 2].astype(jnp.float32)
            for tile in range(8):
                block = volt[feed, :, tile * LANES : (tile + 1) * LANES].astype(jnp.float32) * flag
                raw[tile, pl.ds(pl.multiple_of(feed * pitch + 8, 8), steps), :] = block

    for tile in range(8):
        for back in range(TAPS - 1):
            rows = raw[tile, pl.ds(8 + steps - (TAPS - 1) + back, feeds, stride=pitch), :]
            halo_src[pl.ds(back * feeds, feeds), pl.ds(tile * LANES, LANES)] = rows.astype(jnp.bfloat16)

    def filtered(half):
        first = 4 - 4 * half

        @pl.loop(0, feeds)
        def _(feed):
            station, polar = feed // 2, feed % 2
            for tile in range(8):
                weights = [
                    taps_ref[pl.ds(tap, 1), pl.ds((tile % 4) * LANES, LANES)] for tap in range(TAPS)
                ]
                rows = [
                    raw[tile, pl.ds(feed * pitch + 8 + first - 3 + shift, 8, stride=8), :]
                    for shift in range(7)
                ]
                sums = []
                for index in range(4):
                    total = weights[0] * rows[index]
                    for tap in range(1, TAPS):
                        total = total + weights[tap] * rows[index + tap]
                    sums.append(total)
                block = jnp.concatenate(sums, axis=0).astype(jnp.bfloat16)
                base = station * LANES + polar * 32
                mixed[
                    half, pl.ds(pl.multiple_of(base, 32), 32), tile * LANES : (tile + 1) * LANES
                ] = block
                other = (tile + 4) % 8
                turned = block if tile >= 4 else -block
                mixed[
                    half, pl.ds(pl.multiple_of(base + 64, 32), 32), other * LANES : (other + 1) * LANES
                ] = turned

    depth = 2 * stations

    def transformed(half, pair):
        @pl.loop(0, stations // 2)
        def _(both):
            rows = mixed[half, pl.ds(pl.multiple_of(both * 256, 256), 256), :]
            out = lax.dot_general(
                table[pair * 2 * count : (pair + 1) * 2 * count, :], rows,
                (((1,), (1,)), ((), ())), preferred_element_type=jnp.float32,
            )
            planes[pl.ds(2 * both, 2 * count, stride=stations), :] = out[:, :LANES]
            planes[pl.ds(2 * both + 1, 2 * count, stride=stations), :] = out[:, LANES:]

        group = 16
        slot = 2 * pair + half

        @pl.loop(0, count // group)
        def _(block):
            rows = planes[pl.ds(pl.multiple_of(block * (group * depth), group * depth), group * depth), :]
            a_src[slot, pl.ds(block * group, group)] = rows.astype(jnp.bfloat16).reshape(group, depth, LANES)

    def send_spectra(half, pair):
        slot = 2 * pair + half

        @each_partner
        def _(index):
            pltpu.make_async_remote_copy(
                src_ref=a_src.at[slot, index], dst_ref=a_dst.at[slot, me],
                send_sem=a_send.at[slot], recv_sem=a_recv.at[slot],
                device_id=owner(index), device_id_type=MESH,
            ).start()

        a_dst[slot, me] = a_src[slot, me]

    def await_spectra(half, pair):
        slot = 2 * pair + half
        ref = a_dst.at[slot, pl.ds(0, count - 1)]
        pltpu.make_async_remote_copy(
            src_ref=ref, dst_ref=ref, send_sem=a_send.at[slot], recv_sem=a_recv.at[slot],
            device_id=owner(me), device_id_type=MESH,
        ).wait()

    filtered(0)
    pl.semaphore_wait(barrier, count - 1)

    halo = []
    for back in range(TAPS - 1):
        span = pl.ds(back * feeds, feeds)
        halo.append(
            pltpu.make_async_remote_copy(
                src_ref=halo_src.at[span], dst_ref=halo_dst.at[span],
                send_sem=halo_send.at[back], recv_sem=halo_recv.at[back],
                device_id=(stn, (chan + 1) % chan_count), device_id_type=MESH,
            )
        )
        halo[-1].start()

    table_copy.wait()
    transformed(0, 0)
    send_spectra(0, 0)

    for copy in halo:
        copy.wait()
    for tile in range(8):
        for back in range(TAPS - 1):
            rows = halo_dst[pl.ds(back * feeds, feeds), pl.ds(tile * LANES, LANES)].astype(jnp.float32)
            rows = jnp.where(chan == 0, 0.0, rows)
            raw[tile, pl.ds(8 - (TAPS - 1) + back, feeds, stride=pitch), :] = rows

    filtered(1)
    transformed(1, 0)
    send_spectra(1, 0)
    transformed(0, 1)
    send_spectra(0, 1)
    transformed(1, 1)
    send_spectra(1, 1)

    lane = lax.broadcasted_iota(jnp.int32, (1, LANES), 1)
    first_polar = lane % 64 < 32
    polar_sign = jnp.where(first_polar, 1.0, -1.0)
    turn_sign = jnp.where(lane < 64, 1.0, -1.0)
    rows_total = stn_count * stations

    def correlated(own):
        for half in range(2):
            @pl.loop(0, chan_count)
            def _(source):
                x = jnp.concatenate(
                    [
                        a_dst[
                            2 * (own // 2) + half, block * chan_count + source,
                            own % 2 * stations : (own % 2 + 1) * stations, :,
                        ]
                        for block in range(stn_count)
                    ],
                    axis=0,
                ).astype(jnp.float32)
                swapped = jnp.where(first_polar, pltpu.roll(x, 96, 1), pltpu.roll(x, 32, 1))
                turned = pltpu.roll(x, 64, 1) * turn_sign
                both = pltpu.roll(swapped, 64, 1) * turn_sign
                values = [
                    x, turned, x * polar_sign, turned * polar_sign,
                    swapped, both, both * -polar_sign, swapped * polar_sign,
                ]
                lanes = pl.ds(pl.multiple_of((half * chan_count + source) * LANES, LANES), LANES)
                for index, value in enumerate(values):
                    terms[index * rows_total : (index + 1) * rows_total, lanes] = value.astype(jnp.bfloat16)

        @pl.loop(0, 4)
        def _(quarter):
            left = terms[pl.ds(pl.multiple_of(quarter * 2 * rows_total, 2 * rows_total), 2 * rows_total), :]
            out = lax.dot_general(
                left, terms[:rows_total, :], (((1,), (1,)), ((), ())), preferred_element_type=jnp.float32
            ).astype(jnp.bfloat16)
            for which in range(2):
                rows = out[which * rows_total : (which + 1) * rows_total]
                b_src[own, :, 2 * quarter + which] = rows.reshape(stn_count, stations, rows_total)

    own_copies = []
    for own in range(per_device):
        if own % 2 == 0:
            await_spectra(0, own // 2)
            await_spectra(1, own // 2)
        correlated(own)

        @pl.loop(1, stn_count)
        def _(step):
            target = (stn + step) % stn_count
            pltpu.make_async_remote_copy(
                src_ref=b_src.at[own, target], dst_ref=out_ref.at[stn * per_device + own],
                send_sem=b_send, recv_sem=b_recv, device_id=(target, chan), device_id_type=MESH,
            ).start()

        own_copies.append(
            pltpu.make_async_copy(b_src.at[own, stn], out_ref.at[stn * per_device + own], own_sem.at[own])
        )
        own_copies[-1].start()

    for copy in own_copies:
        copy.wait()
    ref = out_ref.at[pl.ds(0, (stn_count - 1) * per_device)]
    pltpu.make_async_remote_copy(
        src_ref=ref, dst_ref=ref, send_sem=b_send, recv_sem=b_recv,
        device_id=owner(me), device_id_type=MESH,
    ).wait()


def widen(scale, narrow_hbm, wide_hbm, narrow, wide, in_sem, out_sem):
    parts = in_sem.shape[0]
    share = narrow.shape[0] // parts
    spans = [pl.ds(part * share, share) for part in range(parts)]
    loads = [
        pltpu.make_async_copy(narrow_hbm.at[span], narrow.at[span], in_sem.at[part])
        for part, span in enumerate(spans)
    ]
    stores = [
        pltpu.make_async_copy(wide.at[span], wide_hbm.at[span], out_sem.at[part])
        for part, span in enumerate(spans)
    ]
    for load in loads:
        load.start()
    for part in range(parts):
        loads[part].wait()

        @pl.loop(part * share, (part + 1) * share)
        def _(row):
            wide[row] = narrow[row].astype(jnp.float32) * scale

        stores[part].start()
    for store in stores:
        store.wait()


def on_device(voltages, taps, flags):
    stn_count, chan_count = lax.axis_size("stn"), lax.axis_size("chan")
    count = stn_count * chan_count
    stations, polars, steps, width = voltages.shape
    feeds = stations * polars
    per_device = CHANNELS // count
    total = stn_count * stations
    vmem = pltpu.VMEM
    out_dims = (CHANNELS // chan_count, 8, stations, total)
    narrow = pl.pallas_call(
        kernel,
        out_shape=jax.ShapeDtypeStruct(out_dims, jnp.bfloat16),
        in_specs=[
            pl.BlockSpec(memory_space=pl.ANY),
            pl.BlockSpec(memory_space=vmem),
            pl.BlockSpec(memory_space=pltpu.SMEM),
            pl.BlockSpec(memory_space=pl.ANY),
        ],
        out_specs=pl.BlockSpec(memory_space=pl.ANY),
        scratch_shapes=[
            vmem((feeds, steps, width), jnp.bfloat16),
            vmem((CHANNELS, width), jnp.bfloat16),
            vmem((8, feeds * (steps + 8), LANES), jnp.float32),
            vmem((2, stations * LANES, width), jnp.bfloat16),
            vmem((2 * count * stations, LANES), jnp.float32),
            vmem((per_device, count, 2 * stations, LANES), jnp.bfloat16),
            vmem((per_device, count, 2 * stations, LANES), jnp.bfloat16),
            vmem((8 * total, 2 * chan_count * LANES), jnp.bfloat16),
            vmem((per_device, stn_count, 8, stations, total), jnp.bfloat16),
            vmem(((TAPS - 1) * feeds, width), jnp.bfloat16),
            vmem(((TAPS - 1) * feeds, width), jnp.bfloat16),
            pltpu.SemaphoreType.DMA((5,)),
            pltpu.SemaphoreType.DMA((TAPS - 1,)),
            pltpu.SemaphoreType.DMA((TAPS - 1,)),
            pltpu.SemaphoreType.DMA((per_device,)),
            pltpu.SemaphoreType.DMA((per_device,)),
            pltpu.SemaphoreType.DMA,
            pltpu.SemaphoreType.DMA,
            pltpu.SemaphoreType.DMA((per_device,)),
        ],
        compiler_params=pltpu.CompilerParams(
            collective_id=0, has_side_effects=True, vmem_limit_bytes=60 * 1024 * 1024
        ),
        name="correlate",
    )(voltages.reshape(feeds, steps, width), taps, flags, half_table(stn_count, chan_count))
    return pl.pallas_call(
        functools.partial(widen, 1.0 / (steps * chan_count)),
        out_shape=jax.ShapeDtypeStruct(out_dims, jnp.float32),
        in_specs=[pl.BlockSpec(memory_space=pl.ANY)],
        out_specs=pl.BlockSpec(memory_space=pl.ANY),
        scratch_shapes=[
            vmem(out_dims, jnp.bfloat16),
            vmem(out_dims, jnp.float32),
            pltpu.SemaphoreType.DMA((16,)),
            pltpu.SemaphoreType.DMA((16,)),
        ],
        compiler_params=pltpu.CompilerParams(vmem_limit_bytes=60 * 1024 * 1024),
        name="widen",
    )(narrow)


def solution(mesh):
    return jax.shard_map(
        on_device,
        mesh=mesh,
        in_specs=(P("stn", None, "chan", None), P(), P("stn")),
        out_specs=P("chan", None, "stn", None),
        check_vma=False,
    )
```

```python
import functools
import math

import jax
import jax.numpy as jnp
import numpy as np
from jax import lax
from jax.experimental import pallas as pl
from jax.experimental.pallas import tpu as pltpu
from jax.sharding import PartitionSpec as P

CHANNELS = 512
TAPS = 4
LANES = 128
MESH = pl.DeviceIdType.MESH


def half_table(stn_count, chan_count):
    per_device = CHANNELS // (stn_count * chan_count)
    pair, stn, chan, own = np.meshgrid(
        np.arange(per_device // 2), np.arange(stn_count), np.arange(chan_count), np.arange(2), indexing="ij"
    )
    rows = (chan * stn_count * per_device + stn * per_device + pair * 2 + own).reshape(-1)
    turns = (rows[:, None] * np.arange(CHANNELS)[None, :] % CHANNELS).astype(np.float32)
    angles = np.float32(2.0 * math.pi / CHANNELS) * turns
    factor = np.float32(1.0 / math.sqrt(CHANNELS))
    table = np.concatenate([np.cos(angles) * factor, np.sin(angles) * factor], axis=1)
    return jnp.asarray(table.astype(jnp.bfloat16))


def kernel(
    volt_hbm, taps_ref, flags_ref, table_hbm, out_ref,
    volt, table, raw, mixed, planes, a_src, a_dst, terms, b_src, halo_src, halo_dst,
    load_sem, halo_send, halo_recv, a_send, a_recv, b_send, b_recv, own_sem,
):
    stn_count, chan_count = lax.axis_size("stn"), lax.axis_size("chan")
    count = stn_count * chan_count
    stn, chan = lax.axis_index("stn"), lax.axis_index("chan")
    me = stn * chan_count + chan
    feeds, steps = volt.shape[0], volt.shape[1]
    stations = feeds // 2
    pitch = steps + 8
    per_device = CHANNELS // count
    parts = load_sem.shape[0] - 1
    share = feeds // parts

    def owner(index):
        return (index // chan_count, index % chan_count)

    x, z, core, y = stn // 4, (stn // 2 % 2) * 2 + chan // 4, stn % 2, chan % 4
    along_x = [(x + step) % 4 * 32 for step in range(4)]
    along_y = [(y + step) % 4 for step in range(4)]

    def plane_of(outer):
        other_z = (z + outer + 1) % 4
        return other_z // 2 * 16 + other_z % 2 * 4 + (core + outer // 4) % 2 * 8

    def each_partner(act):
        @pl.loop(0, 8)
        def _(outer):
            base = plane_of(outer)
            for step_y in range(4):
                for step_x in range(4):
                    index = base + along_x[step_x] + along_y[step_y]
                    if step_x == 0 and step_y == 0:
                        pl.when(outer != 3)(functools.partial(act, index))
                    else:
                        act(index)

    table_copy = pltpu.make_async_copy(table_hbm, table, load_sem.at[parts])
    loads = []
    for part in range(parts):
        span = pl.ds(part * share, share)
        loads.append(pltpu.make_async_copy(volt_hbm.at[span], volt.at[span], load_sem.at[part]))
        loads[-1].start()
    table_copy.start()

    barrier = pltpu.get_barrier_semaphore()

    def greet(index):
        pl.semaphore_signal(barrier, inc=1, device_id=owner(index), device_id_type=MESH)

    each_partner(greet)

    for part in range(parts):
        loads[part].wait()

        @pl.loop(part * share, (part + 1) * share)
        def _(feed):
            flag = flags_ref[feed // 2].astype(jnp.float32)
            for tile in range(8):
                block = volt[feed, :, tile * LANES : (tile + 1) * LANES].astype(jnp.float32) * flag
                raw[tile, pl.ds(pl.multiple_of(feed * pitch + 8, 8), steps), :] = block

    for tile in range(8):
        for back in range(TAPS - 1):
            rows = raw[tile, pl.ds(8 + steps - (TAPS - 1) + back, feeds, stride=pitch), :]
            halo_src[pl.ds(back * feeds, feeds), pl.ds(tile * LANES, LANES)] = rows.astype(jnp.bfloat16)

    def filtered(half):
        first = 4 - 4 * half

        @pl.loop(0, feeds)
        def _(feed):
            station, polar = feed // 2, feed % 2
            for tile in range(8):
                weights = [
                    taps_ref[pl.ds(tap, 1), pl.ds((tile % 4) * LANES, LANES)] for tap in range(TAPS)
                ]
                rows = [
                    raw[tile, pl.ds(feed * pitch + 8 + first - 3 + shift, 8, stride=8), :]
                    for shift in range(7)
                ]
                sums = []
                for index in range(4):
                    total = weights[0] * rows[index]
                    for tap in range(1, TAPS):
                        total = total + weights[tap] * rows[index + tap]
                    sums.append(total)
                block = jnp.concatenate(sums, axis=0).astype(jnp.bfloat16)
                base = station * LANES + polar * 32
                mixed[
                    half, pl.ds(pl.multiple_of(base, 32), 32), tile * LANES : (tile + 1) * LANES
                ] = block
                other = (tile + 4) % 8
                turned = block if tile >= 4 else -block
                mixed[
                    half, pl.ds(pl.multiple_of(base + 64, 32), 32), other * LANES : (other + 1) * LANES
                ] = turned

    depth = 2 * stations

    def transformed(half, pair):
        @pl.loop(0, stations // 2)
        def _(both):
            rows = mixed[half, pl.ds(pl.multiple_of(both * 256, 256), 256), :]
            out = lax.dot_general(
                table[pair * 2 * count : (pair + 1) * 2 * count, :], rows,
                (((1,), (1,)), ((), ())), preferred_element_type=jnp.float32,
            )
            planes[pl.ds(2 * both, 2 * count, stride=stations), :] = out[:, :LANES]
            planes[pl.ds(2 * both + 1, 2 * count, stride=stations), :] = out[:, LANES:]

        group = 16
        slot = 2 * pair + half

        @pl.loop(0, count // group)
        def _(block):
            rows = planes[pl.ds(pl.multiple_of(block * (group * depth), group * depth), group * depth), :]
            a_src[slot, pl.ds(block * group, group)] = rows.astype(jnp.bfloat16).reshape(group, depth, LANES)

    def send_spectra(half, pair):
        slot = 2 * pair + half

        @each_partner
        def _(index):
            pltpu.make_async_remote_copy(
                src_ref=a_src.at[slot, index], dst_ref=a_dst.at[slot, me],
                send_sem=a_send.at[slot], recv_sem=a_recv.at[slot],
                device_id=owner(index), device_id_type=MESH,
            ).start()

        a_dst[slot, me] = a_src[slot, me]

    def await_spectra(half, pair):
        slot = 2 * pair + half
        ref = a_dst.at[slot, pl.ds(0, count - 1)]
        pltpu.make_async_remote_copy(
            src_ref=ref, dst_ref=ref, send_sem=a_send.at[slot], recv_sem=a_recv.at[slot],
            device_id=owner(me), device_id_type=MESH,
        ).wait()

    filtered(0)
    pl.semaphore_wait(barrier, count - 1)

    halo = []
    for back in range(TAPS - 1):
        span = pl.ds(back * feeds, feeds)
        halo.append(
            pltpu.make_async_remote_copy(
                src_ref=halo_src.at[span], dst_ref=halo_dst.at[span],
                send_sem=halo_send.at[back], recv_sem=halo_recv.at[back],
                device_id=(stn, (chan + 1) % chan_count), device_id_type=MESH,
            )
        )
        halo[-1].start()

    table_copy.wait()
    transformed(0, 0)
    send_spectra(0, 0)

    for copy in halo:
        copy.wait()
    for tile in range(8):
        for back in range(TAPS - 1):
            rows = halo_dst[pl.ds(back * feeds, feeds), pl.ds(tile * LANES, LANES)].astype(jnp.float32)
            rows = jnp.where(chan == 0, 0.0, rows)
            raw[tile, pl.ds(8 - (TAPS - 1) + back, feeds, stride=pitch), :] = rows

    filtered(1)
    transformed(1, 0)
    send_spectra(1, 0)
    transformed(0, 1)
    send_spectra(0, 1)
    transformed(1, 1)
    send_spectra(1, 1)

    lane = lax.broadcasted_iota(jnp.int32, (1, LANES), 1)
    first_polar = lane % 64 < 32
    polar_sign = jnp.where(first_polar, 1.0, -1.0)
    turn_sign = jnp.where(lane < 64, 1.0, -1.0)
    rows_total = stn_count * stations
    targets = [(stn + step) % stn_count for step in range(1, stn_count)]

    def correlated(own):
        for half in range(2):
            @pl.loop(0, chan_count)
            def _(source):
                x = jnp.concatenate(
                    [
                        a_dst[
                            2 * (own // 2) + half, block * chan_count + source,
                            own % 2 * stations : (own % 2 + 1) * stations, :,
                        ]
                        for block in range(stn_count)
                    ],
                    axis=0,
                ).astype(jnp.float32)
                swapped = jnp.where(first_polar, pltpu.roll(x, 96, 1), pltpu.roll(x, 32, 1))
                turned = pltpu.roll(x, 64, 1) * turn_sign
                both = pltpu.roll(swapped, 64, 1) * turn_sign
                values = [
                    x, turned, x * polar_sign, turned * polar_sign,
                    swapped, both, both * -polar_sign, swapped * polar_sign,
                ]
                lanes = pl.ds(pl.multiple_of((half * chan_count + source) * LANES, LANES), LANES)
                for index, value in enumerate(values):
                    terms[index * rows_total : (index + 1) * rows_total, lanes] = value.astype(jnp.bfloat16)

        @pl.loop(0, 4)
        def _(quarter):
            left = terms[pl.ds(pl.multiple_of(quarter * 2 * rows_total, 2 * rows_total), 2 * rows_total), :]
            out = lax.dot_general(
                left, terms[:rows_total, :], (((1,), (1,)), ((), ())), preferred_element_type=jnp.float32
            ).astype(jnp.bfloat16)
            for which in range(2):
                rows = out[which * rows_total : (which + 1) * rows_total]
                b_src[own, :, 2 * quarter + which] = rows.reshape(stn_count, stations, rows_total)
            for which in range(2):
                for target in targets:
                    pltpu.make_async_remote_copy(
                        src_ref=b_src.at[own, target, 2 * quarter + which],
                        dst_ref=out_ref.at[stn * per_device + own, 2 * quarter + which],
                        send_sem=b_send, recv_sem=b_recv, device_id=(target, chan), device_id_type=MESH,
                    ).start()

    own_copies = []
    for own in range(per_device):
        if own % 2 == 0:
            await_spectra(0, own // 2)
            await_spectra(1, own // 2)
        correlated(own)

        own_copies.append(
            pltpu.make_async_copy(b_src.at[own, stn], out_ref.at[stn * per_device + own], own_sem.at[own])
        )
        own_copies[-1].start()

    for copy in own_copies:
        copy.wait()
    ref = out_ref.at[pl.ds(0, (stn_count - 1) * per_device)]
    pltpu.make_async_remote_copy(
        src_ref=ref, dst_ref=ref, send_sem=b_send, recv_sem=b_recv,
        device_id=owner(me), device_id_type=MESH,
    ).wait()


def widen(scale, narrow_hbm, wide_hbm, narrow, wide, in_sem, out_sem):
    parts = in_sem.shape[0]
    share = narrow.shape[0] // parts
    spans = [pl.ds(part * share, share) for part in range(parts)]
    loads = [
        pltpu.make_async_copy(narrow_hbm.at[span], narrow.at[span], in_sem.at[part])
        for part, span in enumerate(spans)
    ]
    stores = [
        pltpu.make_async_copy(wide.at[span], wide_hbm.at[span], out_sem.at[part])
        for part, span in enumerate(spans)
    ]
    for load in loads:
        load.start()
    for part in range(parts):
        loads[part].wait()

        @pl.loop(part * share, (part + 1) * share)
        def _(row):
            wide[row] = narrow[row].astype(jnp.float32) * scale

        stores[part].start()
    for store in stores:
        store.wait()


def on_device(voltages, taps, flags):
    stn_count, chan_count = lax.axis_size("stn"), lax.axis_size("chan")
    count = stn_count * chan_count
    stations, polars, steps, width = voltages.shape
    feeds = stations * polars
    per_device = CHANNELS // count
    total = stn_count * stations
    vmem = pltpu.VMEM
    out_dims = (CHANNELS // chan_count, 8, stations, total)
    narrow = pl.pallas_call(
        kernel,
        out_shape=jax.ShapeDtypeStruct(out_dims, jnp.bfloat16),
        in_specs=[
            pl.BlockSpec(memory_space=pl.ANY),
            pl.BlockSpec(memory_space=vmem),
            pl.BlockSpec(memory_space=pltpu.SMEM),
            pl.BlockSpec(memory_space=pl.ANY),
        ],
        out_specs=pl.BlockSpec(memory_space=pl.ANY),
        scratch_shapes=[
            vmem((feeds, steps, width), jnp.bfloat16),
            vmem((CHANNELS, width), jnp.bfloat16),
            vmem((8, feeds * (steps + 8), LANES), jnp.float32),
            vmem((2, stations * LANES, width), jnp.bfloat16),
            vmem((2 * count * stations, LANES), jnp.float32),
            vmem((per_device, count, 2 * stations, LANES), jnp.bfloat16),
            vmem((per_device, count, 2 * stations, LANES), jnp.bfloat16),
            vmem((8 * total, 2 * chan_count * LANES), jnp.bfloat16),
            vmem((per_device, stn_count, 8, stations, total), jnp.bfloat16),
            vmem(((TAPS - 1) * feeds, width), jnp.bfloat16),
            vmem(((TAPS - 1) * feeds, width), jnp.bfloat16),
            pltpu.SemaphoreType.DMA((5,)),
            pltpu.SemaphoreType.DMA((TAPS - 1,)),
            pltpu.SemaphoreType.DMA((TAPS - 1,)),
            pltpu.SemaphoreType.DMA((per_device,)),
            pltpu.SemaphoreType.DMA((per_device,)),
            pltpu.SemaphoreType.DMA,
            pltpu.SemaphoreType.DMA,
            pltpu.SemaphoreType.DMA((per_device,)),
        ],
        compiler_params=pltpu.CompilerParams(
            collective_id=0, has_side_effects=True, vmem_limit_bytes=60 * 1024 * 1024
        ),
        name="correlate",
    )(voltages.reshape(feeds, steps, width), taps, flags, half_table(stn_count, chan_count))
    return pl.pallas_call(
        functools.partial(widen, 1.0 / (steps * chan_count)),
        out_shape=jax.ShapeDtypeStruct(out_dims, jnp.float32),
        in_specs=[pl.BlockSpec(memory_space=pl.ANY)],
        out_specs=pl.BlockSpec(memory_space=pl.ANY),
        scratch_shapes=[
            vmem(out_dims, jnp.bfloat16),
            vmem(out_dims, jnp.float32),
            pltpu.SemaphoreType.DMA((16,)),
            pltpu.SemaphoreType.DMA((16,)),
        ],
        compiler_params=pltpu.CompilerParams(vmem_limit_bytes=60 * 1024 * 1024),
        name="widen",
    )(narrow)


def solution(mesh):
    return jax.shard_map(
        on_device,
        mesh=mesh,
        in_specs=(P("stn", None, "chan", None), P(), P("stn")),
        out_specs=P("chan", None, "stn", None),
        check_vma=False,
    )
```

```python
import functools
import math

import jax
import jax.numpy as jnp
import numpy as np
from jax import lax
from jax.experimental import pallas as pl
from jax.experimental.pallas import tpu as pltpu
from jax.sharding import PartitionSpec as P

CHANNELS = 512
TAPS = 4
LANES = 128
MESH = pl.DeviceIdType.MESH


def half_table(stn_count, chan_count):
    per_device = CHANNELS // (stn_count * chan_count)
    pair, stn, chan, own = np.meshgrid(
        np.arange(per_device // 2), np.arange(stn_count), np.arange(chan_count), np.arange(2), indexing="ij"
    )
    rows = (chan * stn_count * per_device + stn * per_device + pair * 2 + own).reshape(-1)
    turns = (rows[:, None] * np.arange(CHANNELS)[None, :] % CHANNELS).astype(np.float32)
    angles = np.float32(2.0 * math.pi / CHANNELS) * turns
    factor = np.float32(1.0 / math.sqrt(CHANNELS))
    table = np.concatenate([np.cos(angles) * factor, np.sin(angles) * factor], axis=1)
    return jnp.asarray(table.astype(jnp.bfloat16))


def kernel(
    volt_hbm, taps_ref, flags_ref, table_hbm, out_ref,
    volt, table, raw, mixed, planes, a_src, a_dst, terms, b_src, halo_src, halo_dst,
    load_sem, halo_send, halo_recv, a_send, a_recv, b_send, b_recv, own_sem,
):
    stn_count, chan_count = lax.axis_size("stn"), lax.axis_size("chan")
    count = stn_count * chan_count
    stn, chan = lax.axis_index("stn"), lax.axis_index("chan")
    me = stn * chan_count + chan
    feeds, steps = volt.shape[0], volt.shape[1]
    stations = feeds // 2
    pitch = steps + 8
    per_device = CHANNELS // count
    parts = load_sem.shape[0] - 1
    share = feeds // parts

    def owner(index):
        return (index // chan_count, index % chan_count)

    x, z, core, y = stn // 4, (stn // 2 % 2) * 2 + chan // 4, stn % 2, chan % 4
    along_x = [(x + step) % 4 * 32 for step in range(4)]
    along_y = [(y + step) % 4 for step in range(4)]

    def plane_of(outer):
        other_z = (z + outer + 1) % 4
        return other_z // 2 * 16 + other_z % 2 * 4 + (core + outer // 4) % 2 * 8

    def each_partner(act):
        @pl.loop(0, 8)
        def _(outer):
            base = plane_of(outer)
            for step_y in range(4):
                for step_x in range(4):
                    index = base + along_x[step_x] + along_y[step_y]
                    if step_x == 0 and step_y == 0:
                        pl.when(outer != 3)(functools.partial(act, index))
                    else:
                        act(index)

    table_copy = pltpu.make_async_copy(table_hbm, table, load_sem.at[parts])
    loads = []
    for part in range(parts):
        span = pl.ds(part * share, share)
        loads.append(pltpu.make_async_copy(volt_hbm.at[span], volt.at[span], load_sem.at[part]))
        loads[-1].start()
    table_copy.start()

    barrier = pltpu.get_barrier_semaphore()

    def greet(index):
        pl.semaphore_signal(barrier, inc=1, device_id=owner(index), device_id_type=MESH)

    each_partner(greet)

    for part in range(parts):
        loads[part].wait()

        @pl.loop(part * share, (part + 1) * share)
        def _(feed):
            flag = flags_ref[feed // 2].astype(jnp.float32)
            for tile in range(8):
                block = volt[feed, :, tile * LANES : (tile + 1) * LANES].astype(jnp.float32) * flag
                raw[tile, pl.ds(pl.multiple_of(feed * pitch + 8, 8), steps), :] = block

    for tile in range(8):
        for back in range(TAPS - 1):
            rows = raw[tile, pl.ds(8 + steps - (TAPS - 1) + back, feeds, stride=pitch), :]
            halo_src[pl.ds(back * feeds, feeds), pl.ds(tile * LANES, LANES)] = rows.astype(jnp.bfloat16)

    def filtered(half):
        first = 4 - 4 * half

        @pl.loop(0, feeds)
        def _(feed):
            station, polar = feed // 2, feed % 2
            for tile in range(8):
                weights = [
                    taps_ref[pl.ds(tap, 1), pl.ds((tile % 4) * LANES, LANES)] for tap in range(TAPS)
                ]
                rows = [
                    raw[tile, pl.ds(feed * pitch + 8 + first - 3 + shift, 8, stride=8), :]
                    for shift in range(7)
                ]
                sums = []
                for index in range(4):
                    total = weights[0] * rows[index]
                    for tap in range(1, TAPS):
                        total = total + weights[tap] * rows[index + tap]
                    sums.append(total)
                block = jnp.concatenate(sums, axis=0).astype(jnp.bfloat16)
                base = station * LANES + polar * 32
                mixed[
                    half, pl.ds(pl.multiple_of(base, 32), 32), tile * LANES : (tile + 1) * LANES
                ] = block
                other = (tile + 4) % 8
                turned = block if tile >= 4 else -block
                mixed[
                    half, pl.ds(pl.multiple_of(base + 64, 32), 32), other * LANES : (other + 1) * LANES
                ] = turned

    depth = 2 * stations

    def transformed(half, pair):
        @pl.loop(0, stations // 2)
        def _(both):
            rows = mixed[half, pl.ds(pl.multiple_of(both * 256, 256), 256), :]
            out = lax.dot_general(
                table[pair * 2 * count : (pair + 1) * 2 * count, :], rows,
                (((1,), (1,)), ((), ())), preferred_element_type=jnp.float32,
            )
            planes[pl.ds(2 * both, 2 * count, stride=stations), :] = out[:, :LANES]
            planes[pl.ds(2 * both + 1, 2 * count, stride=stations), :] = out[:, LANES:]

        group = 16
        slot = 2 * pair + half

        @pl.loop(0, count // group)
        def _(block):
            rows = planes[pl.ds(pl.multiple_of(block * (group * depth), group * depth), group * depth), :]
            a_src[slot, pl.ds(block * group, group)] = rows.astype(jnp.bfloat16).reshape(group, depth, LANES)

    def send_spectra(half, pair):
        slot = 2 * pair + half

        @each_partner
        def _(index):
            pltpu.make_async_remote_copy(
                src_ref=a_src.at[slot, index], dst_ref=a_dst.at[slot, me],
                send_sem=a_send.at[slot], recv_sem=a_recv.at[slot],
                device_id=owner(index), device_id_type=MESH,
            ).start()

        a_dst[slot, me] = a_src[slot, me]

    def await_spectra(half, pair):
        slot = 2 * pair + half
        ref = a_dst.at[slot, pl.ds(0, count - 1)]
        pltpu.make_async_remote_copy(
            src_ref=ref, dst_ref=ref, send_sem=a_send.at[slot], recv_sem=a_recv.at[slot],
            device_id=owner(me), device_id_type=MESH,
        ).wait()

    pl.semaphore_wait(barrier, count - 1)

    has_next, has_last = chan < chan_count - 1, chan > 0
    halo = []
    for back in range(TAPS - 1):
        span = pl.ds(back * feeds, feeds)
        halo.append(
            pltpu.make_async_remote_copy(
                src_ref=halo_src.at[span], dst_ref=halo_dst.at[span],
                send_sem=halo_send.at[back], recv_sem=halo_recv.at[back],
                device_id=(stn, (chan + 1) % chan_count), device_id_type=MESH,
            )
        )
        pl.when(has_next)(halo[-1].start)

    filtered(0)
    table_copy.wait()
    transformed(0, 0)
    send_spectra(0, 0)

    for copy in halo:
        pl.when(has_next)(copy.wait_send)

    @pl.when(has_last)
    def _():
        for copy in halo:
            copy.wait_recv()
        for tile in range(8):
            for back in range(TAPS - 1):
                rows = halo_dst[pl.ds(back * feeds, feeds), pl.ds(tile * LANES, LANES)]
                raw[tile, pl.ds(8 - (TAPS - 1) + back, feeds, stride=pitch), :] = rows.astype(jnp.float32)

    @pl.when(jnp.logical_not(has_last))
    def _():
        for tile in range(8):
            for back in range(TAPS - 1):
                raw[tile, pl.ds(8 - (TAPS - 1) + back, feeds, stride=pitch), :] = jnp.zeros(
                    (feeds, LANES), jnp.float32
                )

    filtered(1)
    transformed(1, 0)
    send_spectra(1, 0)
    transformed(0, 1)
    send_spectra(0, 1)
    transformed(1, 1)
    send_spectra(1, 1)

    lane = lax.broadcasted_iota(jnp.int32, (1, LANES), 1)
    first_polar = lane % 64 < 32
    polar_sign = jnp.where(first_polar, 1.0, -1.0)
    turn_sign = jnp.where(lane < 64, 1.0, -1.0)
    rows_total = stn_count * stations
    targets = [(stn + step) % stn_count for step in range(1, stn_count)]

    def correlated(own):
        for half in range(2):
            @pl.loop(0, chan_count)
            def _(source):
                x = jnp.concatenate(
                    [
                        a_dst[
                            2 * (own // 2) + half, block * chan_count + source,
                            own % 2 * stations : (own % 2 + 1) * stations, :,
                        ]
                        for block in range(stn_count)
                    ],
                    axis=0,
                ).astype(jnp.float32)
                swapped = jnp.where(first_polar, pltpu.roll(x, 96, 1), pltpu.roll(x, 32, 1))
                turned = pltpu.roll(x, 64, 1) * turn_sign
                both = pltpu.roll(swapped, 64, 1) * turn_sign
                values = [
                    x, turned, x * polar_sign, turned * polar_sign,
                    swapped, both, both * -polar_sign, swapped * polar_sign,
                ]
                lanes = pl.ds(pl.multiple_of((half * chan_count + source) * LANES, LANES), LANES)
                for index, value in enumerate(values):
                    terms[index * rows_total : (index + 1) * rows_total, lanes] = value.astype(jnp.bfloat16)

        @pl.loop(0, 4)
        def _(quarter):
            left = terms[pl.ds(pl.multiple_of(quarter * 2 * rows_total, 2 * rows_total), 2 * rows_total), :]
            out = lax.dot_general(
                left, terms[:rows_total, :], (((1,), (1,)), ((), ())), preferred_element_type=jnp.float32
            ).astype(jnp.bfloat16)
            for which in range(2):
                rows = out[which * rows_total : (which + 1) * rows_total]
                b_src[own, :, 2 * quarter + which] = rows.reshape(stn_count, stations, rows_total)
            for which in range(2):
                for target in targets:
                    pltpu.make_async_remote_copy(
                        src_ref=b_src.at[own, target, 2 * quarter + which],
                        dst_ref=out_ref.at[stn * per_device + own, 2 * quarter + which],
                        send_sem=b_send, recv_sem=b_recv, device_id=(target, chan), device_id_type=MESH,
                    ).start()

    own_copies = []
    for own in range(per_device):
        if own % 2 == 0:
            await_spectra(0, own // 2)
            await_spectra(1, own // 2)
        correlated(own)

        own_copies.append(
            pltpu.make_async_copy(b_src.at[own, stn], out_ref.at[stn * per_device + own], own_sem.at[own])
        )
        own_copies[-1].start()

    for copy in own_copies:
        copy.wait()
    ref = out_ref.at[pl.ds(0, (stn_count - 1) * per_device)]
    pltpu.make_async_remote_copy(
        src_ref=ref, dst_ref=ref, send_sem=b_send, recv_sem=b_recv,
        device_id=owner(me), device_id_type=MESH,
    ).wait()


def widen(scale, narrow, wide_hbm, wide, out_sem):
    parts = out_sem.shape[0]
    share = narrow.shape[0] // parts
    stores = []
    for part in range(parts):
        @pl.loop(part * share, (part + 1) * share)
        def _(row):
            wide[row] = narrow[row].astype(jnp.float32) * scale

        span = pl.ds(part * share, share)
        stores.append(pltpu.make_async_copy(wide.at[span], wide_hbm.at[span], out_sem.at[part]))
        stores[-1].start()
    for store in stores:
        store.wait()


def on_device(voltages, taps, flags):
    stn_count, chan_count = lax.axis_size("stn"), lax.axis_size("chan")
    count = stn_count * chan_count
    stations, polars, steps, width = voltages.shape
    feeds = stations * polars
    per_device = CHANNELS // count
    total = stn_count * stations
    vmem = pltpu.VMEM
    out_dims = (CHANNELS // chan_count, 8, stations, total)
    narrow = pl.pallas_call(
        kernel,
        out_shape=vmem(out_dims, jnp.bfloat16),
        in_specs=[
            pl.BlockSpec(memory_space=pltpu.HBM),
            pl.BlockSpec(memory_space=vmem),
            pl.BlockSpec(memory_space=pltpu.SMEM),
            pl.BlockSpec(memory_space=pltpu.HBM),
        ],
        out_specs=pl.BlockSpec(memory_space=vmem),
        scratch_shapes=[
            vmem((feeds, steps, width), jnp.bfloat16),
            vmem((CHANNELS, width), jnp.bfloat16),
            vmem((8, feeds * (steps + 8), LANES), jnp.float32),
            vmem((2, stations * LANES, width), jnp.bfloat16),
            vmem((2 * count * stations, LANES), jnp.float32),
            vmem((per_device, count, 2 * stations, LANES), jnp.bfloat16),
            vmem((per_device, count, 2 * stations, LANES), jnp.bfloat16),
            vmem((8 * total, 2 * chan_count * LANES), jnp.bfloat16),
            vmem((per_device, stn_count, 8, stations, total), jnp.bfloat16),
            vmem(((TAPS - 1) * feeds, width), jnp.bfloat16),
            vmem(((TAPS - 1) * feeds, width), jnp.bfloat16),
            pltpu.SemaphoreType.DMA((5,)),
            pltpu.SemaphoreType.DMA((TAPS - 1,)),
            pltpu.SemaphoreType.DMA((TAPS - 1,)),
            pltpu.SemaphoreType.DMA((per_device,)),
            pltpu.SemaphoreType.DMA((per_device,)),
            pltpu.SemaphoreType.DMA,
            pltpu.SemaphoreType.DMA,
            pltpu.SemaphoreType.DMA((per_device,)),
        ],
        compiler_params=pltpu.CompilerParams(
            collective_id=0, has_side_effects=True, vmem_limit_bytes=50 * 1024 * 1024
        ),
        name="correlate",
    )(voltages.reshape(feeds, steps, width), taps, flags, half_table(stn_count, chan_count))
    return pl.pallas_call(
        functools.partial(widen, 1.0 / (steps * chan_count)),
        out_shape=jax.ShapeDtypeStruct(out_dims, jnp.float32),
        in_specs=[pl.BlockSpec(memory_space=vmem)],
        out_specs=pl.BlockSpec(memory_space=pl.ANY),
        scratch_shapes=[
            vmem(out_dims, jnp.float32),
            pltpu.SemaphoreType.DMA((16,)),
        ],
        compiler_params=pltpu.CompilerParams(vmem_limit_bytes=16 * 1024 * 1024),
        name="widen",
    )(narrow)


def solution(mesh):
    return jax.shard_map(
        on_device,
        mesh=mesh,
        in_specs=(P("stn", None, "chan", None), P(), P("stn")),
        out_specs=P("chan", None, "stn", None),
        check_vma=False,
    )
```

```python
import functools
import math

import jax
import jax.numpy as jnp
import numpy as np
from jax import lax
from jax.experimental import pallas as pl
from jax.experimental.pallas import tpu as pltpu
from jax.sharding import PartitionSpec as P

CHANNELS = 512
TAPS = 4
LANES = 128
MESH = pl.DeviceIdType.MESH


def half_table(stn_count, chan_count):
    per_device = CHANNELS // (stn_count * chan_count)
    pair, stn, chan, own = np.meshgrid(
        np.arange(per_device // 2), np.arange(stn_count), np.arange(chan_count), np.arange(2), indexing="ij"
    )
    rows = (chan * stn_count * per_device + stn * per_device + pair * 2 + own).reshape(-1)
    turns = (rows[:, None] * np.arange(CHANNELS)[None, :] % CHANNELS).astype(np.float32)
    angles = np.float32(2.0 * math.pi / CHANNELS) * turns
    factor = np.float32(1.0 / math.sqrt(CHANNELS))
    table = np.concatenate([np.cos(angles) * factor, np.sin(angles) * factor], axis=1)
    return jnp.asarray(table.astype(jnp.bfloat16))


def kernel(
    volt_hbm, taps_ref, flags_ref, table_hbm, out_ref,
    volt, table, raw, mixed, planes, a_src, a_dst, terms, b_src, halo_src, halo_dst,
    load_sem, halo_send, halo_recv, a_send, a_recv, b_send, b_recv, own_sem,
):
    stn_count, chan_count = lax.axis_size("stn"), lax.axis_size("chan")
    count = stn_count * chan_count
    stn, chan = lax.axis_index("stn"), lax.axis_index("chan")
    me = stn * chan_count + chan
    feeds, steps = volt.shape[0], volt.shape[1]
    stations = feeds // 2
    pitch = steps + 8
    per_device = CHANNELS // count
    parts = load_sem.shape[0] - 1
    share = feeds // parts

    def owner(index):
        return (index // chan_count, index % chan_count)

    x, z, core, y = stn // 4, (stn // 2 % 2) * 2 + chan // 4, stn % 2, chan % 4
    along_x = [(x + step) % 4 * 32 for step in range(4)]
    along_y = [(y + step) % 4 for step in range(4)]

    def plane_of(outer):
        other_z = (z + outer + 1) % 4
        return other_z // 2 * 16 + other_z % 2 * 4 + (core + outer // 4) % 2 * 8

    def each_partner(act):
        @pl.loop(0, 8)
        def _(outer):
            base = plane_of(outer)
            for step_y in range(4):
                for step_x in range(4):
                    index = base + along_x[step_x] + along_y[step_y]
                    if step_x == 0 and step_y == 0:
                        pl.when(outer != 3)(functools.partial(act, index))
                    else:
                        act(index)

    table_copy = pltpu.make_async_copy(table_hbm, table, load_sem.at[parts])
    loads = []
    for part in range(parts):
        span = pl.ds(part * share, share)
        loads.append(pltpu.make_async_copy(volt_hbm.at[span], volt.at[span], load_sem.at[part]))
        loads[-1].start()
    table_copy.start()

    barrier = pltpu.get_barrier_semaphore()

    def greet(index):
        pl.semaphore_signal(barrier, inc=1, device_id=owner(index), device_id_type=MESH)

    each_partner(greet)

    for part in range(parts):
        loads[part].wait()

        @pl.loop(part * share, (part + 1) * share)
        def _(feed):
            flag = flags_ref[feed // 2].astype(jnp.float32)
            for tile in range(8):
                block = volt[feed, :, tile * LANES : (tile + 1) * LANES].astype(jnp.float32) * flag
                raw[tile, pl.ds(pl.multiple_of(feed * pitch + 8, 8), steps), :] = block

    for tile in range(8):
        for back in range(TAPS - 1):
            rows = raw[tile, pl.ds(8 + steps - (TAPS - 1) + back, feeds, stride=pitch), :]
            halo_src[pl.ds(back * feeds, feeds), pl.ds(tile * LANES, LANES)] = rows.astype(jnp.bfloat16)

    def filtered(half, both):
        first = 4 - 4 * half
        for feed_of in range(4):
            feed = 4 * both + feed_of
            for tile in range(8):
                weights = [
                    taps_ref[pl.ds(tap, 1), pl.ds((tile % 4) * LANES, LANES)] for tap in range(TAPS)
                ]
                rows = [
                    raw[tile, pl.ds(feed * pitch + 8 + first - 3 + shift, 8, stride=8), :]
                    for shift in range(7)
                ]
                sums = []
                for index in range(4):
                    total = weights[0] * rows[index]
                    for tap in range(1, TAPS):
                        total = total + weights[tap] * rows[index + tap]
                    sums.append(total)
                block = jnp.concatenate(sums, axis=0).astype(jnp.bfloat16)
                base = both * 2 * LANES + feed_of // 2 * LANES + feed_of % 2 * 32
                mixed[
                    half, pl.ds(pl.multiple_of(base, 32), 32), tile * LANES : (tile + 1) * LANES
                ] = block
                other = (tile + 4) % 8
                turned = block if tile >= 4 else -block
                mixed[
                    half, pl.ds(pl.multiple_of(base + 64, 32), 32), other * LANES : (other + 1) * LANES
                ] = turned

    depth = 2 * stations

    def transformed(half, pair, both):
        rows = mixed[half, pl.ds(pl.multiple_of(both * 256, 256), 256), :]
        out = lax.dot_general(
            table[pair * 2 * count : (pair + 1) * 2 * count, :], rows,
            (((1,), (1,)), ((), ())), preferred_element_type=jnp.float32,
        )
        planes[pl.ds(2 * both, 2 * count, stride=stations), :] = out[:, :LANES]
        planes[pl.ds(2 * both + 1, 2 * count, stride=stations), :] = out[:, LANES:]

    def packed(half, pair):
        group = 16
        slot = 2 * pair + half

        @pl.loop(0, count // group)
        def _(block):
            rows = planes[pl.ds(pl.multiple_of(block * (group * depth), group * depth), group * depth), :]
            a_src[slot, pl.ds(block * group, group)] = rows.astype(jnp.bfloat16).reshape(group, depth, LANES)

    def first_spectra(half):
        last = stations // 2 - 1
        filtered(half, 0)

        @pl.loop(0, last)
        def _(both):
            transformed(half, 0, both)
            filtered(half, both + 1)

        transformed(half, 0, last)
        packed(half, 0)

    def second_spectra(half):
        @pl.loop(0, stations // 2)
        def _(both):
            transformed(half, 1, both)

        packed(half, 1)

    def send_spectra(half, pair):
        slot = 2 * pair + half

        @each_partner
        def _(index):
            pltpu.make_async_remote_copy(
                src_ref=a_src.at[slot, index], dst_ref=a_dst.at[slot, me],
                send_sem=a_send.at[slot], recv_sem=a_recv.at[slot],
                device_id=owner(index), device_id_type=MESH,
            ).start()

        a_dst[slot, me] = a_src[slot, me]

    def await_spectra(half, pair):
        slot = 2 * pair + half
        ref = a_dst.at[slot, pl.ds(0, count - 1)]
        pltpu.make_async_remote_copy(
            src_ref=ref, dst_ref=ref, send_sem=a_send.at[slot], recv_sem=a_recv.at[slot],
            device_id=owner(me), device_id_type=MESH,
        ).wait()

    pl.semaphore_wait(barrier, count - 1)

    has_next, has_last = chan < chan_count - 1, chan > 0
    halo = []
    for back in range(TAPS - 1):
        span = pl.ds(back * feeds, feeds)
        halo.append(
            pltpu.make_async_remote_copy(
                src_ref=halo_src.at[span], dst_ref=halo_dst.at[span],
                send_sem=halo_send.at[back], recv_sem=halo_recv.at[back],
                device_id=(stn, (chan + 1) % chan_count), device_id_type=MESH,
            )
        )
        pl.when(has_next)(halo[-1].start)

    table_copy.wait()
    first_spectra(0)
    send_spectra(0, 0)

    for copy in halo:
        pl.when(has_next)(copy.wait_send)

    @pl.when(has_last)
    def _():
        for copy in halo:
            copy.wait_recv()
        for tile in range(8):
            for back in range(TAPS - 1):
                rows = halo_dst[pl.ds(back * feeds, feeds), pl.ds(tile * LANES, LANES)]
                raw[tile, pl.ds(8 - (TAPS - 1) + back, feeds, stride=pitch), :] = rows.astype(jnp.float32)

    @pl.when(jnp.logical_not(has_last))
    def _():
        for tile in range(8):
            for back in range(TAPS - 1):
                raw[tile, pl.ds(8 - (TAPS - 1) + back, feeds, stride=pitch), :] = jnp.zeros(
                    (feeds, LANES), jnp.float32
                )

    first_spectra(1)
    send_spectra(1, 0)
    second_spectra(0)
    send_spectra(0, 1)
    second_spectra(1)
    send_spectra(1, 1)

    lane = lax.broadcasted_iota(jnp.int32, (1, LANES), 1)
    first_part = lane % 64 < 32
    turn_sign = jnp.where(lane < 64, 1.0, -1.0)
    rows_total = stn_count * stations
    targets = [(stn + step) % stn_count for step in range(1, stn_count)]

    def correlated(own):
        for half in range(2):
            @pl.loop(0, chan_count // 2)
            def _(couple):
                first, second = (
                    jnp.concatenate(
                        [
                            a_dst[
                                2 * (own // 2) + half, block * chan_count + 2 * couple + source,
                                own % 2 * stations : (own % 2 + 1) * stations, :,
                            ]
                            for block in range(stn_count)
                        ],
                        axis=0,
                    ).astype(jnp.float32)
                    for source in range(2)
                )
                polars = [
                    jnp.where(first_part, first, pltpu.roll(second, 32, 1)),
                    jnp.where(first_part, pltpu.roll(first, 96, 1), second),
                ]
                lanes = pl.ds(pl.multiple_of((half * (chan_count // 2) + couple) * LANES, LANES), LANES)
                for polar, value in enumerate(polars):
                    turned = pltpu.roll(value, 64, 1) * turn_sign
                    terms[polar * rows_total : (polar + 1) * rows_total, lanes] = value.astype(jnp.bfloat16)
                    terms[(2 + polar) * rows_total : (3 + polar) * rows_total, lanes] = turned.astype(jnp.bfloat16)

        for part in range(2):
            out = lax.dot_general(
                terms[part * 2 * rows_total : (part + 1) * 2 * rows_total, :], terms[: 2 * rows_total, :],
                (((1,), (1,)), ((), ())), preferred_element_type=jnp.float32,
            )
            xx, xy = out[:rows_total, :rows_total], out[:rows_total, rows_total:]
            yx, yy = out[rows_total:, :rows_total], out[rows_total:, rows_total:]
            stokes = [
                (part, xx + yy), (2 + part, xx - yy), (4 + part, xy + yx),
                (7, yx - xy) if part == 0 else (6, xy - yx),
            ]
            for index, value in stokes:
                b_src[own, :, index] = value.astype(jnp.bfloat16).reshape(stn_count, stations, rows_total)
            for index, _ in stokes:
                for target in targets:
                    pltpu.make_async_remote_copy(
                        src_ref=b_src.at[own, target, index],
                        dst_ref=out_ref.at[stn * per_device + own, index],
                        send_sem=b_send, recv_sem=b_recv, device_id=(target, chan), device_id_type=MESH,
                    ).start()

    own_copies = []
    for own in range(per_device):
        if own % 2 == 0:
            await_spectra(0, own // 2)
            await_spectra(1, own // 2)
        correlated(own)

        own_copies.append(
            pltpu.make_async_copy(b_src.at[own, stn], out_ref.at[stn * per_device + own], own_sem.at[own])
        )
        own_copies[-1].start()

    for copy in own_copies:
        copy.wait()
    ref = out_ref.at[pl.ds(0, (stn_count - 1) * per_device)]
    pltpu.make_async_remote_copy(
        src_ref=ref, dst_ref=ref, send_sem=b_send, recv_sem=b_recv,
        device_id=owner(me), device_id_type=MESH,
    ).wait()


def widen(scale, narrow, wide_hbm, wide, out_sem):
    parts = out_sem.shape[0]
    share = narrow.shape[0] // parts
    stores = []
    for part in range(parts):
        @pl.loop(part * share, (part + 1) * share)
        def _(row):
            wide[row] = narrow[row].astype(jnp.float32) * scale

        span = pl.ds(part * share, share)
        stores.append(pltpu.make_async_copy(wide.at[span], wide_hbm.at[span], out_sem.at[part]))
        stores[-1].start()
    for store in stores:
        store.wait()


def on_device(voltages, taps, flags):
    stn_count, chan_count = lax.axis_size("stn"), lax.axis_size("chan")
    count = stn_count * chan_count
    stations, polars, steps, width = voltages.shape
    feeds = stations * polars
    per_device = CHANNELS // count
    total = stn_count * stations
    vmem = pltpu.VMEM
    out_dims = (CHANNELS // chan_count, 8, stations, total)
    narrow = pl.pallas_call(
        kernel,
        out_shape=vmem(out_dims, jnp.bfloat16),
        in_specs=[
            pl.BlockSpec(memory_space=pltpu.HBM),
            pl.BlockSpec(memory_space=vmem),
            pl.BlockSpec(memory_space=pltpu.SMEM),
            pl.BlockSpec(memory_space=pltpu.HBM),
        ],
        out_specs=pl.BlockSpec(memory_space=vmem),
        scratch_shapes=[
            vmem((feeds, steps, width), jnp.bfloat16),
            vmem((CHANNELS, width), jnp.bfloat16),
            vmem((8, feeds * (steps + 8), LANES), jnp.float32),
            vmem((2, stations * LANES, width), jnp.bfloat16),
            vmem((2 * count * stations, LANES), jnp.float32),
            vmem((per_device, count, 2 * stations, LANES), jnp.bfloat16),
            vmem((per_device, count, 2 * stations, LANES), jnp.bfloat16),
            vmem((4 * total, chan_count * LANES), jnp.bfloat16),
            vmem((per_device, stn_count, 8, stations, total), jnp.bfloat16),
            vmem(((TAPS - 1) * feeds, width), jnp.bfloat16),
            vmem(((TAPS - 1) * feeds, width), jnp.bfloat16),
            pltpu.SemaphoreType.DMA((5,)),
            pltpu.SemaphoreType.DMA((TAPS - 1,)),
            pltpu.SemaphoreType.DMA((TAPS - 1,)),
            pltpu.SemaphoreType.DMA((per_device,)),
            pltpu.SemaphoreType.DMA((per_device,)),
            pltpu.SemaphoreType.DMA,
            pltpu.SemaphoreType.DMA,
            pltpu.SemaphoreType.DMA((per_device,)),
        ],
        compiler_params=pltpu.CompilerParams(
            collective_id=0, has_side_effects=True, vmem_limit_bytes=50 * 1024 * 1024
        ),
        name="correlate",
    )(voltages.reshape(feeds, steps, width), taps, flags, half_table(stn_count, chan_count))
    return pl.pallas_call(
        functools.partial(widen, 1.0 / (steps * chan_count)),
        out_shape=jax.ShapeDtypeStruct(out_dims, jnp.float32),
        in_specs=[pl.BlockSpec(memory_space=vmem)],
        out_specs=pl.BlockSpec(memory_space=pl.ANY),
        scratch_shapes=[
            vmem(out_dims, jnp.float32),
            pltpu.SemaphoreType.DMA((16,)),
        ],
        compiler_params=pltpu.CompilerParams(vmem_limit_bytes=16 * 1024 * 1024),
        name="widen",
    )(narrow)


def solution(mesh):
    return jax.shard_map(
        on_device,
        mesh=mesh,
        in_specs=(P("stn", None, "chan", None), P(), P("stn")),
        out_specs=P("chan", None, "stn", None),
        check_vma=False,
    )
```

```python
import functools
import math

import jax
import jax.numpy as jnp
import numpy as np
from jax import lax
from jax.experimental import pallas as pl
from jax.experimental.pallas import tpu as pltpu
from jax.sharding import PartitionSpec as P

CHANNELS = 512
TAPS = 4
LANES = 128
MESH = pl.DeviceIdType.MESH


def half_table(stn_count, chan_count):
    per_device = CHANNELS // (stn_count * chan_count)
    pair, stn, chan, own = np.meshgrid(
        np.arange(per_device // 2), np.arange(stn_count), np.arange(chan_count), np.arange(2), indexing="ij"
    )
    rows = (chan * stn_count * per_device + stn * per_device + pair * 2 + own).reshape(-1)
    turns = (rows[:, None] * np.arange(CHANNELS)[None, :] % CHANNELS).astype(np.float32)
    angles = np.float32(2.0 * math.pi / CHANNELS) * turns
    factor = np.float32(1.0 / math.sqrt(CHANNELS))
    table = np.concatenate([np.cos(angles) * factor, np.sin(angles) * factor], axis=1)
    return jnp.asarray(table.astype(jnp.bfloat16))


def kernel(
    volt_hbm, taps_hbm, flags_hbm, table_hbm, out_ref,
    taps_ref, flags_ref, volt, table, raw, mixed_even, mixed_odd, planes, a_src, a_dst, terms, b_src, halo_src, halo_dst,
    load_sem, halo_send, halo_recv, a_send, a_recv, b_send, b_recv, own_sem,
):
    stn_count, chan_count = lax.axis_size("stn"), lax.axis_size("chan")
    count = stn_count * chan_count
    stn, chan = lax.axis_index("stn"), lax.axis_index("chan")
    me = stn * chan_count + chan
    feeds, steps = volt.shape[0], volt.shape[1]
    stations = feeds // 2
    pitch = steps + 8
    per_device = CHANNELS // count
    parts = load_sem.shape[0] - 3
    share = feeds // parts

    def owner(index):
        return (index // chan_count, index % chan_count)

    x, z, core, y = stn // 4, (stn // 2 % 2) * 2 + chan // 4, stn % 2, chan % 4
    along_x = [(x + step) % 4 * 32 for step in range(4)]
    along_y = [(y + step) % 4 for step in range(4)]

    def plane_of(outer):
        other_z = (z + outer + 1) % 4
        return other_z // 2 * 16 + other_z % 2 * 4 + (core + outer // 4) % 2 * 8

    def each_partner(act):
        @pl.loop(0, 8)
        def _(outer):
            base = plane_of(outer)
            for step_y in range(4):
                for step_x in range(4):
                    index = base + along_x[step_x] + along_y[step_y]
                    if step_x == 0 and step_y == 0:
                        pl.when(outer != 3)(functools.partial(act, index))
                    else:
                        act(index)

    table_copy = pltpu.make_async_copy(table_hbm, table, load_sem.at[parts])
    loads = []
    for part in range(parts):
        span = pl.ds(part * share, share)
        loads.append(pltpu.make_async_copy(volt_hbm.at[span], volt.at[span], load_sem.at[part]))
        loads[-1].start()
    small_copies = [
        pltpu.make_async_copy(taps_hbm, taps_ref, load_sem.at[parts + 1]),
        pltpu.make_async_copy(flags_hbm, flags_ref, load_sem.at[parts + 2]),
    ]
    for copy in small_copies:
        copy.start()
    table_copy.start()

    barrier = pltpu.get_barrier_semaphore()

    def greet(index):
        pl.semaphore_signal(barrier, inc=1, device_id=owner(index), device_id_type=MESH)

    each_partner(greet)

    for copy in loads + small_copies:
        copy.wait()

    def widened(feed, start, rows):
        flag = flags_ref[feed // 2].astype(jnp.float32)
        for tile in range(8):
            block = volt[feed, start : start + rows, tile * LANES : (tile + 1) * LANES].astype(jnp.float32)
            raw[tile, pl.ds(pl.multiple_of(feed * pitch + 8 + start, 8), rows), :] = block * flag

    @pl.loop(0, feeds)
    def _(feed):
        widened(feed, steps - 16, 16)

    for tile in range(8):
        for back in range(TAPS - 1):
            rows = raw[tile, pl.ds(8 + steps - (TAPS - 1) + back, feeds, stride=pitch), :]
            halo_src[pl.ds(back * feeds, feeds), pl.ds(tile * LANES, LANES)] = rows.astype(jnp.bfloat16)

    mixed_of = (mixed_even, mixed_odd)

    def filtered(half, both, odd):
        first = 4 - 4 * half
        for feed_of in range(4):
            feed = 4 * both + feed_of
            if half == 0:
                widened(feed, 0, steps - 16)
            for tile in range(8):
                weights = [
                    taps_ref[pl.ds(tap, 1), pl.ds((tile % 4) * LANES, LANES)] for tap in range(TAPS)
                ]
                rows = [
                    raw[tile, pl.ds(feed * pitch + 8 + first - 3 + shift, 8, stride=8), :]
                    for shift in range(7)
                ]
                sums = []
                for index in range(4):
                    total = weights[0] * rows[index]
                    for tap in range(1, TAPS):
                        total = total + weights[tap] * rows[index + tap]
                    sums.append(total)
                block = jnp.concatenate(sums, axis=0).astype(jnp.bfloat16)
                base = both // 2 * 2 * LANES + feed_of // 2 * LANES + feed_of % 2 * 32
                mixed_of[odd][
                    half, pl.ds(pl.multiple_of(base, 32), 32), tile * LANES : (tile + 1) * LANES
                ] = block
                other = (tile + 4) % 8
                turned = block if tile >= 4 else -block
                mixed_of[odd][
                    half, pl.ds(pl.multiple_of(base + 64, 32), 32), other * LANES : (other + 1) * LANES
                ] = turned

    depth = 2 * stations

    def transformed(half, pair, both, odd):
        rows = mixed_of[odd][half, pl.ds(pl.multiple_of(both // 2 * 256, 256), 256), :]
        out = lax.dot_general(
            table[pair * 2 * count : (pair + 1) * 2 * count, :], rows,
            (((1,), (1,)), ((), ())), preferred_element_type=jnp.float32,
        )
        planes[pl.ds(2 * both, 2 * count, stride=stations), :] = out[:, :LANES]
        planes[pl.ds(2 * both + 1, 2 * count, stride=stations), :] = out[:, LANES:]

    def packed(half, pair):
        group = 16
        slot = 2 * pair + half

        @pl.loop(0, count // group)
        def _(block):
            rows = planes[pl.ds(pl.multiple_of(block * (group * depth), group * depth), group * depth), :]
            a_src[slot, pl.ds(block * group, group)] = rows.astype(jnp.bfloat16).reshape(group, depth, LANES)

    def first_spectra(half):
        last = stations // 2 - 1
        filtered(half, 0, 0)

        @pl.loop(0, last // 2)
        def _(step):
            for odd in range(2):
                transformed(half, 0, 2 * step + odd, odd)
                filtered(half, 2 * step + odd + 1, 1 - odd)

        transformed(half, 0, last - 1, 0)
        filtered(half, last, 1)
        transformed(half, 0, last, 1)
        packed(half, 0)

    def second_spectra(half):
        @pl.loop(0, stations // 4)
        def _(step):
            for odd in range(2):
                transformed(half, 1, 2 * step + odd, odd)

        packed(half, 1)

    def send_spectra(half, pair):
        slot = 2 * pair + half

        @each_partner
        def _(index):
            pltpu.make_async_remote_copy(
                src_ref=a_src.at[slot, index], dst_ref=a_dst.at[slot, me],
                send_sem=a_send.at[slot], recv_sem=a_recv.at[slot],
                device_id=owner(index), device_id_type=MESH,
            ).start()

        a_dst[slot, me] = a_src[slot, me]

    def await_spectra(half, pair):
        slot = 2 * pair + half
        ref = a_dst.at[slot, pl.ds(0, count - 1)]
        pltpu.make_async_remote_copy(
            src_ref=ref, dst_ref=ref, send_sem=a_send.at[slot], recv_sem=a_recv.at[slot],
            device_id=owner(me), device_id_type=MESH,
        ).wait()

    pl.semaphore_wait(barrier, count - 1)

    has_next, has_last = chan < chan_count - 1, chan > 0
    halo = []
    for back in range(TAPS - 1):
        span = pl.ds(back * feeds, feeds)
        halo.append(
            pltpu.make_async_remote_copy(
                src_ref=halo_src.at[span], dst_ref=halo_dst.at[span],
                send_sem=halo_send.at[back], recv_sem=halo_recv.at[back],
                device_id=(stn, (chan + 1) % chan_count), device_id_type=MESH,
            )
        )
        pl.when(has_next)(halo[-1].start)

    table_copy.wait()
    first_spectra(0)
    send_spectra(0, 0)

    for copy in halo:
        pl.when(has_next)(copy.wait_send)

    @pl.when(has_last)
    def _():
        for copy in halo:
            copy.wait_recv()
        for tile in range(8):
            for back in range(TAPS - 1):
                rows = halo_dst[pl.ds(back * feeds, feeds), pl.ds(tile * LANES, LANES)]
                raw[tile, pl.ds(8 - (TAPS - 1) + back, feeds, stride=pitch), :] = rows.astype(jnp.float32)

    @pl.when(jnp.logical_not(has_last))
    def _():
        for tile in range(8):
            for back in range(TAPS - 1):
                raw[tile, pl.ds(8 - (TAPS - 1) + back, feeds, stride=pitch), :] = jnp.zeros(
                    (feeds, LANES), jnp.float32
                )

    first_spectra(1)
    send_spectra(1, 0)
    second_spectra(0)
    send_spectra(0, 1)
    second_spectra(1)
    send_spectra(1, 1)

    lane = lax.broadcasted_iota(jnp.int32, (1, LANES), 1)
    first_part = lane % 64 < 32
    turn_sign = jnp.where(lane < 64, 1.0, -1.0)
    rows_total = stn_count * stations
    targets = [(stn + step) % stn_count for step in range(1, stn_count)]

    def correlated(own):
        for half in range(2):
            @pl.loop(0, chan_count // 2)
            def _(couple):
                first, second = (
                    jnp.concatenate(
                        [
                            a_dst[
                                2 * (own // 2) + half, block * chan_count + 2 * couple + source,
                                own % 2 * stations : (own % 2 + 1) * stations, :,
                            ]
                            for block in range(stn_count)
                        ],
                        axis=0,
                    ).astype(jnp.float32)
                    for source in range(2)
                )
                polars = [
                    jnp.where(first_part, first, pltpu.roll(second, 32, 1)),
                    jnp.where(first_part, pltpu.roll(first, 96, 1), second),
                ]
                lanes = pl.ds(pl.multiple_of((half * (chan_count // 2) + couple) * LANES, LANES), LANES)
                for polar, value in enumerate(polars):
                    turned = pltpu.roll(value, 64, 1) * turn_sign
                    terms[polar * rows_total : (polar + 1) * rows_total, lanes] = value.astype(jnp.bfloat16)
                    terms[(2 + polar) * rows_total : (3 + polar) * rows_total, lanes] = turned.astype(jnp.bfloat16)

        for part in range(2):
            out = lax.dot_general(
                terms[part * 2 * rows_total : (part + 1) * 2 * rows_total, :], terms[: 2 * rows_total, :],
                (((1,), (1,)), ((), ())), preferred_element_type=jnp.float32,
            )
            xx, xy = out[:rows_total, :rows_total], out[:rows_total, rows_total:]
            yx, yy = out[rows_total:, :rows_total], out[rows_total:, rows_total:]
            stokes = [
                (part, xx + yy), (2 + part, xx - yy), (4 + part, xy + yx),
                (7, yx - xy) if part == 0 else (6, xy - yx),
            ]
            for index, value in stokes:
                b_src[own, :, index] = value.astype(jnp.bfloat16).reshape(stn_count, stations, rows_total)
            for index, _ in stokes:
                for target in targets:
                    pltpu.make_async_remote_copy(
                        src_ref=b_src.at[own, target, index],
                        dst_ref=out_ref.at[stn * per_device + own, index],
                        send_sem=b_send, recv_sem=b_recv, device_id=(target, chan), device_id_type=MESH,
                    ).start()

    own_copies = []
    for own in range(per_device):
        if own % 2 == 0:
            await_spectra(0, own // 2)
            await_spectra(1, own // 2)
        correlated(own)

        own_copies.append(
            pltpu.make_async_copy(b_src.at[own, stn], out_ref.at[stn * per_device + own], own_sem.at[own])
        )
        own_copies[-1].start()

    for copy in own_copies:
        copy.wait()
    ref = out_ref.at[pl.ds(0, (stn_count - 1) * per_device)]
    pltpu.make_async_remote_copy(
        src_ref=ref, dst_ref=ref, send_sem=b_send, recv_sem=b_recv,
        device_id=owner(me), device_id_type=MESH,
    ).wait()


def widen(scale, narrow, wide_hbm, wide, out_sem):
    parts = out_sem.shape[0]
    share = narrow.shape[0] // parts
    stores = []
    for part in range(parts):
        @pl.loop(part * share, (part + 1) * share)
        def _(row):
            wide[row] = narrow[row].astype(jnp.float32) * scale

        span = pl.ds(part * share, share)
        stores.append(pltpu.make_async_copy(wide.at[span], wide_hbm.at[span], out_sem.at[part]))
        stores[-1].start()
    for store in stores:
        store.wait()


def on_device(voltages, taps, flags):
    stn_count, chan_count = lax.axis_size("stn"), lax.axis_size("chan")
    count = stn_count * chan_count
    stations, polars, steps, width = voltages.shape
    feeds = stations * polars
    per_device = CHANNELS // count
    total = stn_count * stations
    vmem = pltpu.VMEM
    out_dims = (CHANNELS // chan_count, 8, stations, total)
    narrow = pl.pallas_call(
        kernel,
        out_shape=vmem(out_dims, jnp.bfloat16),
        in_specs=[
            pl.BlockSpec(memory_space=pltpu.HBM),
            pl.BlockSpec(memory_space=pltpu.HBM),
            pl.BlockSpec(memory_space=pltpu.HBM),
            pl.BlockSpec(memory_space=pltpu.HBM),
        ],
        out_specs=pl.BlockSpec(memory_space=vmem),
        scratch_shapes=[
            vmem(taps.shape, jnp.float32),
            pltpu.SMEM(flags.shape, jnp.int32),
            vmem((feeds, steps, width), jnp.bfloat16),
            vmem((CHANNELS, width), jnp.bfloat16),
            vmem((8, feeds * (steps + 8), LANES), jnp.float32),
            vmem((2, stations // 2 * LANES, width), jnp.bfloat16),
            vmem((2, stations // 2 * LANES, width), jnp.bfloat16),
            vmem((2 * count * stations, LANES), jnp.float32),
            vmem((per_device, count, 2 * stations, LANES), jnp.bfloat16),
            vmem((per_device, count, 2 * stations, LANES), jnp.bfloat16),
            vmem((4 * total, chan_count * LANES), jnp.bfloat16),
            vmem((per_device, stn_count, 8, stations, total), jnp.bfloat16),
            vmem(((TAPS - 1) * feeds, width), jnp.bfloat16),
            vmem(((TAPS - 1) * feeds, width), jnp.bfloat16),
            pltpu.SemaphoreType.DMA((7,)),
            pltpu.SemaphoreType.DMA((TAPS - 1,)),
            pltpu.SemaphoreType.DMA((TAPS - 1,)),
            pltpu.SemaphoreType.DMA((per_device,)),
            pltpu.SemaphoreType.DMA((per_device,)),
            pltpu.SemaphoreType.DMA,
            pltpu.SemaphoreType.DMA,
            pltpu.SemaphoreType.DMA((per_device,)),
        ],
        compiler_params=pltpu.CompilerParams(
            collective_id=0, has_side_effects=True, vmem_limit_bytes=50 * 1024 * 1024
        ),
        name="correlate",
    )(voltages.reshape(feeds, steps, width), taps, flags, half_table(stn_count, chan_count))
    return pl.pallas_call(
        functools.partial(widen, 1.0 / (steps * chan_count)),
        out_shape=jax.ShapeDtypeStruct(out_dims, jnp.float32),
        in_specs=[pl.BlockSpec(memory_space=vmem)],
        out_specs=pl.BlockSpec(memory_space=pl.ANY),
        scratch_shapes=[
            vmem(out_dims, jnp.float32),
            pltpu.SemaphoreType.DMA((16,)),
        ],
        compiler_params=pltpu.CompilerParams(vmem_limit_bytes=16 * 1024 * 1024),
        name="widen",
    )(narrow)


def solution(mesh):
    return jax.shard_map(
        on_device,
        mesh=mesh,
        in_specs=(P("stn", None, "chan", None), P(), P("stn")),
        out_specs=P("chan", None, "stn", None),
        check_vma=False,
    )
```

```python
import functools
import math

import jax
import jax.numpy as jnp
import numpy as np
from jax import lax
from jax.experimental import pallas as pl
from jax.experimental.pallas import tpu as pltpu
from jax.sharding import PartitionSpec as P

CHANNELS = 512
TAPS = 4
LANES = 128
MESH = pl.DeviceIdType.MESH


def half_table(stn_count, chan_count):
    per_device = CHANNELS // (stn_count * chan_count)
    pair, stn, chan, own = np.meshgrid(
        np.arange(per_device // 2), np.arange(stn_count), np.arange(chan_count), np.arange(2), indexing="ij"
    )
    rows = (chan * stn_count * per_device + stn * per_device + pair * 2 + own).reshape(-1)
    turns = (rows[:, None] * np.arange(CHANNELS)[None, :] % CHANNELS).astype(np.float32)
    angles = np.float32(2.0 * math.pi / CHANNELS) * turns
    factor = np.float32(1.0 / math.sqrt(CHANNELS))
    table = np.concatenate([np.cos(angles) * factor, np.sin(angles) * factor], axis=1)
    return jnp.asarray(table.astype(jnp.bfloat16))


def kernel(
    volt_hbm, taps_hbm, flags_hbm, table_hbm, out_ref,
    taps_ref, flags_ref, volt, table, raw, mixed_even, mixed_odd, planes, a_src, a_dst, terms, b_src, halo_src, halo_dst,
    load_sem, halo_send, halo_recv, a_send, a_recv, b_send, b_recv, own_sem,
):
    stn_count, chan_count = lax.axis_size("stn"), lax.axis_size("chan")
    count = stn_count * chan_count
    stn, chan = lax.axis_index("stn"), lax.axis_index("chan")
    me = stn * chan_count + chan
    feeds, steps = volt.shape[0], volt.shape[1]
    stations = feeds // 2
    pitch = steps + 8
    per_device = CHANNELS // count
    parts = load_sem.shape[0] - 3
    share = feeds // parts

    def owner(index):
        return (index // chan_count, index % chan_count)

    x, z, core, y = stn // 4, (stn // 2 % 2) * 2 + chan // 4, stn % 2, chan % 4
    along_x = [(x + step) % 4 * 32 for step in range(4)]
    along_y = [(y + step) % 4 for step in range(4)]

    def plane_of(outer):
        other_z = (z + outer + 1) % 4
        return other_z // 2 * 16 + other_z % 2 * 4 + (core + outer // 4) % 2 * 8

    def each_partner(act):
        @pl.loop(0, 8)
        def _(outer):
            base = plane_of(outer)
            for step_y in range(4):
                for step_x in range(4):
                    index = base + along_x[step_x] + along_y[step_y]
                    if step_x == 0 and step_y == 0:
                        pl.when(outer != 3)(functools.partial(act, index))
                    else:
                        act(index)

    table_copy = pltpu.make_async_copy(table_hbm, table, load_sem.at[parts])
    loads = []
    for part in range(parts):
        span = pl.ds(part * share, share)
        loads.append(pltpu.make_async_copy(volt_hbm.at[span], volt.at[span], load_sem.at[part]))
        loads[-1].start()
    small_copies = [
        pltpu.make_async_copy(taps_hbm, taps_ref, load_sem.at[parts + 1]),
        pltpu.make_async_copy(flags_hbm, flags_ref, load_sem.at[parts + 2]),
    ]
    for copy in small_copies:
        copy.start()
    table_copy.start()

    barrier = pltpu.get_barrier_semaphore()

    def greet(index):
        pl.semaphore_signal(barrier, inc=1, device_id=owner(index), device_id_type=MESH)

    each_partner(greet)

    for copy in loads + small_copies:
        copy.wait()

    def widened(feed, start, rows):
        flag = flags_ref[feed // 2].astype(jnp.float32)
        for tile in range(8):
            block = volt[feed, start : start + rows, tile * LANES : (tile + 1) * LANES].astype(jnp.float32)
            raw[tile, pl.ds(pl.multiple_of(feed * pitch + 8 + start, 8), rows), :] = block * flag

    @pl.loop(0, feeds)
    def _(feed):
        widened(feed, steps - 16, 16)

    for tile in range(8):
        for back in range(TAPS - 1):
            rows = raw[tile, pl.ds(8 + steps - (TAPS - 1) + back, feeds, stride=pitch), :]
            halo_src[pl.ds(back * feeds, feeds), pl.ds(tile * LANES, LANES)] = rows.astype(jnp.bfloat16)

    mixed_of = (mixed_even, mixed_odd)

    def filtered(half, both, odd):
        first = 4 - 4 * half
        for feed_of in range(4):
            feed = 4 * both + feed_of
            if half == 0:
                widened(feed, 0, steps - 16)
            for tile in range(8):
                weights = [
                    taps_ref[pl.ds(tap, 1), pl.ds((tile % 4) * LANES, LANES)] for tap in range(TAPS)
                ]
                rows = [
                    raw[tile, pl.ds(feed * pitch + 8 + first - 3 + shift, 8, stride=8), :]
                    for shift in range(7)
                ]
                sums = []
                for index in range(4):
                    total = weights[0] * rows[index]
                    for tap in range(1, TAPS):
                        total = total + weights[tap] * rows[index + tap]
                    sums.append(total)
                block = jnp.concatenate(sums, axis=0).astype(jnp.bfloat16)
                base = both // 2 * 2 * LANES + feed_of // 2 * LANES + feed_of % 2 * 32
                mixed_of[odd][
                    half, pl.ds(pl.multiple_of(base, 32), 32), tile * LANES : (tile + 1) * LANES
                ] = block
                other = (tile + 4) % 8
                turned = block if tile >= 4 else -block
                mixed_of[odd][
                    half, pl.ds(pl.multiple_of(base + 64, 32), 32), other * LANES : (other + 1) * LANES
                ] = turned

    depth = 2 * stations

    def transformed(half, pair, both, odd):
        rows = mixed_of[odd][half, pl.ds(pl.multiple_of(both // 2 * 256, 256), 256), :]
        out = lax.dot_general(
            table[pair * 2 * count : (pair + 1) * 2 * count, :], rows,
            (((1,), (1,)), ((), ())), preferred_element_type=jnp.float32,
        )
        planes[pl.ds(2 * both, 2 * count, stride=stations), :] = out[:, :LANES]
        planes[pl.ds(2 * both + 1, 2 * count, stride=stations), :] = out[:, LANES:]

    def packed(index):
        rows = planes[pl.ds(pl.multiple_of(index * depth, depth), depth), :]
        return rows.astype(jnp.bfloat16)

    def first_spectra(half):
        last = stations // 2 - 1
        filtered(half, 0, 0)

        @pl.loop(0, last // 2)
        def _(step):
            for odd in range(2):
                transformed(half, 0, 2 * step + odd, odd)
                filtered(half, 2 * step + odd + 1, 1 - odd)

        transformed(half, 0, last - 1, 0)
        filtered(half, last, 1)
        transformed(half, 0, last, 1)

    def second_spectra(half):
        @pl.loop(0, stations // 4)
        def _(step):
            for odd in range(2):
                transformed(half, 1, 2 * step + odd, odd)

    def send_spectra(half, pair):
        slot = 2 * pair + half

        @each_partner
        def _(index):
            a_src[slot, index] = packed(index)
            pltpu.make_async_remote_copy(
                src_ref=a_src.at[slot, index], dst_ref=a_dst.at[slot, me],
                send_sem=a_send.at[slot], recv_sem=a_recv.at[slot],
                device_id=owner(index), device_id_type=MESH,
            ).start()

        a_dst[slot, me] = packed(me)

    def all_spectra(half, pair):
        slot = 2 * pair + half
        ref = a_dst.at[slot, pl.ds(0, count - 1)]
        return pltpu.make_async_remote_copy(
            src_ref=ref, dst_ref=ref, send_sem=a_send.at[slot], recv_sem=a_recv.at[slot],
            device_id=owner(me), device_id_type=MESH,
        )

    pl.semaphore_wait(barrier, count - 1)

    has_next, has_last = chan < chan_count - 1, chan > 0
    halo = []
    for back in range(TAPS - 1):
        span = pl.ds(back * feeds, feeds)
        halo.append(
            pltpu.make_async_remote_copy(
                src_ref=halo_src.at[span], dst_ref=halo_dst.at[span],
                send_sem=halo_send.at[back], recv_sem=halo_recv.at[back],
                device_id=(stn, (chan + 1) % chan_count), device_id_type=MESH,
            )
        )
        pl.when(has_next)(halo[-1].start)

    table_copy.wait()
    first_spectra(0)
    send_spectra(0, 0)

    @pl.when(has_last)
    def _():
        for copy in halo:
            copy.wait_recv()
        for tile in range(8):
            for back in range(TAPS - 1):
                rows = halo_dst[pl.ds(back * feeds, feeds), pl.ds(tile * LANES, LANES)]
                raw[tile, pl.ds(8 - (TAPS - 1) + back, feeds, stride=pitch), :] = rows.astype(jnp.float32)

    @pl.when(jnp.logical_not(has_last))
    def _():
        for tile in range(8):
            for back in range(TAPS - 1):
                raw[tile, pl.ds(8 - (TAPS - 1) + back, feeds, stride=pitch), :] = jnp.zeros(
                    (feeds, LANES), jnp.float32
                )

    first_spectra(1)
    send_spectra(1, 0)
    second_spectra(0)
    send_spectra(0, 1)
    second_spectra(1)
    send_spectra(1, 1)

    lane = lax.broadcasted_iota(jnp.int32, (1, LANES), 1)
    first_part = lane % 64 < 32
    turn_sign = jnp.where(lane < 64, 1.0, -1.0)
    rows_total = stn_count * stations
    targets = [(stn + step) % stn_count for step in range(1, stn_count)]

    def correlated(own):
        for half in range(2):
            @pl.loop(0, chan_count // 2)
            def _(couple):
                first, second = (
                    jnp.concatenate(
                        [
                            a_dst[
                                2 * (own // 2) + half, block * chan_count + 2 * couple + source,
                                own % 2 * stations : (own % 2 + 1) * stations, :,
                            ]
                            for block in range(stn_count)
                        ],
                        axis=0,
                    ).astype(jnp.float32)
                    for source in range(2)
                )
                polars = [
                    jnp.where(first_part, first, pltpu.roll(second, 32, 1)),
                    jnp.where(first_part, pltpu.roll(first, 96, 1), second),
                ]
                lanes = pl.ds(pl.multiple_of((half * (chan_count // 2) + couple) * LANES, LANES), LANES)
                for polar, value in enumerate(polars):
                    turned = pltpu.roll(value, 64, 1) * turn_sign
                    terms[polar * rows_total : (polar + 1) * rows_total, lanes] = value.astype(jnp.bfloat16)
                    terms[(2 + polar) * rows_total : (3 + polar) * rows_total, lanes] = turned.astype(jnp.bfloat16)

        for part in range(2):
            out = lax.dot_general(
                terms[part * 2 * rows_total : (part + 1) * 2 * rows_total, :], terms[: 2 * rows_total, :],
                (((1,), (1,)), ((), ())), preferred_element_type=jnp.float32,
            )
            xx, xy = out[:rows_total, :rows_total], out[:rows_total, rows_total:]
            yx, yy = out[rows_total:, :rows_total], out[rows_total:, rows_total:]
            stokes = [
                (part, xx + yy), (2 + part, xx - yy), (4 + part, xy + yx),
                (7, yx - xy) if part == 0 else (6, xy - yx),
            ]
            for index, value in stokes:
                b_src[own, :, index] = value.astype(jnp.bfloat16).reshape(stn_count, stations, rows_total)
            for index, _ in stokes:
                for target in targets:
                    pltpu.make_async_remote_copy(
                        src_ref=b_src.at[own, target, index],
                        dst_ref=out_ref.at[stn * per_device + own, index],
                        send_sem=b_send, recv_sem=b_recv, device_id=(target, chan), device_id_type=MESH,
                    ).start()

    own_copies = []
    for own in range(per_device):
        if own % 2 == 0:
            all_spectra(0, own // 2).wait_recv()
            all_spectra(1, own // 2).wait_recv()
        correlated(own)

        own_copies.append(
            pltpu.make_async_copy(b_src.at[own, stn], out_ref.at[stn * per_device + own], own_sem.at[own])
        )
        own_copies[-1].start()

    for copy in halo:
        pl.when(has_next)(copy.wait_send)
    for pair in range(per_device // 2):
        for half in range(2):
            all_spectra(half, pair).wait_send()
    for copy in own_copies:
        copy.wait()
    ref = out_ref.at[pl.ds(0, (stn_count - 1) * per_device)]
    pltpu.make_async_remote_copy(
        src_ref=ref, dst_ref=ref, send_sem=b_send, recv_sem=b_recv,
        device_id=owner(me), device_id_type=MESH,
    ).wait()


def widen(scale, narrow, wide_hbm, wide, out_sem):
    parts = out_sem.shape[0]
    share = narrow.shape[0] // parts
    stores = []
    for part in range(parts):
        @pl.loop(part * share, (part + 1) * share)
        def _(row):
            wide[row] = narrow[row].astype(jnp.float32) * scale

        span = pl.ds(part * share, share)
        stores.append(pltpu.make_async_copy(wide.at[span], wide_hbm.at[span], out_sem.at[part]))
        stores[-1].start()
    for store in stores:
        store.wait()


def on_device(voltages, taps, flags):
    stn_count, chan_count = lax.axis_size("stn"), lax.axis_size("chan")
    count = stn_count * chan_count
    stations, polars, steps, width = voltages.shape
    feeds = stations * polars
    per_device = CHANNELS // count
    total = stn_count * stations
    vmem = pltpu.VMEM
    out_dims = (CHANNELS // chan_count, 8, stations, total)
    narrow = pl.pallas_call(
        kernel,
        out_shape=vmem(out_dims, jnp.bfloat16),
        in_specs=[
            pl.BlockSpec(memory_space=pltpu.HBM),
            pl.BlockSpec(memory_space=pltpu.HBM),
            pl.BlockSpec(memory_space=pltpu.HBM),
            pl.BlockSpec(memory_space=pltpu.HBM),
        ],
        out_specs=pl.BlockSpec(memory_space=vmem),
        scratch_shapes=[
            vmem(taps.shape, jnp.float32),
            pltpu.SMEM(flags.shape, jnp.int32),
            vmem((feeds, steps, width), jnp.bfloat16),
            vmem((CHANNELS, width), jnp.bfloat16),
            vmem((8, feeds * (steps + 8), LANES), jnp.float32),
            vmem((2, stations // 2 * LANES, width), jnp.bfloat16),
            vmem((2, stations // 2 * LANES, width), jnp.bfloat16),
            vmem((2 * count * stations, LANES), jnp.float32),
            vmem((per_device, count, 2 * stations, LANES), jnp.bfloat16),
            vmem((per_device, count, 2 * stations, LANES), jnp.bfloat16),
            vmem((4 * total, chan_count * LANES), jnp.bfloat16),
            vmem((per_device, stn_count, 8, stations, total), jnp.bfloat16),
            vmem(((TAPS - 1) * feeds, width), jnp.bfloat16),
            vmem(((TAPS - 1) * feeds, width), jnp.bfloat16),
            pltpu.SemaphoreType.DMA((7,)),
            pltpu.SemaphoreType.DMA((TAPS - 1,)),
            pltpu.SemaphoreType.DMA((TAPS - 1,)),
            pltpu.SemaphoreType.DMA((per_device,)),
            pltpu.SemaphoreType.DMA((per_device,)),
            pltpu.SemaphoreType.DMA,
            pltpu.SemaphoreType.DMA,
            pltpu.SemaphoreType.DMA((per_device,)),
        ],
        compiler_params=pltpu.CompilerParams(
            collective_id=0, has_side_effects=True, vmem_limit_bytes=50 * 1024 * 1024
        ),
        name="correlate",
    )(voltages.reshape(feeds, steps, width), taps, flags, half_table(stn_count, chan_count))
    return pl.pallas_call(
        functools.partial(widen, 1.0 / (steps * chan_count)),
        out_shape=jax.ShapeDtypeStruct(out_dims, jnp.float32),
        in_specs=[pl.BlockSpec(memory_space=vmem)],
        out_specs=pl.BlockSpec(memory_space=pl.ANY),
        scratch_shapes=[
            vmem(out_dims, jnp.float32),
            pltpu.SemaphoreType.DMA((16,)),
        ],
        compiler_params=pltpu.CompilerParams(vmem_limit_bytes=16 * 1024 * 1024),
        name="widen",
    )(narrow)


def solution(mesh):
    return jax.shard_map(
        on_device,
        mesh=mesh,
        in_specs=(P("stn", None, "chan", None), P(), P("stn")),
        out_specs=P("chan", None, "stn", None),
        check_vma=False,
    )
```

```python
import functools
import math

import jax
import jax.numpy as jnp
import numpy as np
from jax import lax
from jax.experimental import pallas as pl
from jax.experimental.pallas import tpu as pltpu
from jax.sharding import PartitionSpec as P

CHANNELS = 512
TAPS = 4
LANES = 128
MESH = pl.DeviceIdType.MESH


def half_table(stn_count, chan_count):
    per_device = CHANNELS // (stn_count * chan_count)
    pair, stn, chan, own = np.meshgrid(
        np.arange(per_device // 2), np.arange(stn_count), np.arange(chan_count), np.arange(2), indexing="ij"
    )
    rows = (chan * stn_count * per_device + stn * per_device + pair * 2 + own).reshape(-1)
    turns = (rows[:, None] * np.arange(CHANNELS)[None, :] % CHANNELS).astype(np.float32)
    angles = np.float32(2.0 * math.pi / CHANNELS) * turns
    factor = np.float32(1.0 / math.sqrt(CHANNELS))
    table = np.concatenate([np.cos(angles) * factor, np.sin(angles) * factor], axis=1)
    return jnp.asarray(table.astype(jnp.bfloat16))


def kernel(
    volt_hbm, taps_hbm, flags_hbm, table_hbm, out_ref,
    taps_ref, flags_ref, volt, table, raw, mixed_even, mixed_odd, planes, a_src, a_dst, terms, b_src, halo_src, halo_dst,
    load_sem, halo_send, halo_recv, a_send, a_recv, b_send, b_recv, own_sem,
):
    stn_count, chan_count = lax.axis_size("stn"), lax.axis_size("chan")
    count = stn_count * chan_count
    stn, chan = lax.axis_index("stn"), lax.axis_index("chan")
    me = stn * chan_count + chan
    feeds, steps = volt.shape[0], volt.shape[1]
    stations = feeds // 2
    pitch = steps + 8
    per_device = CHANNELS // count
    parts = load_sem.shape[0] - 3
    share = feeds // parts

    def owner(index):
        return (index // chan_count, index % chan_count)

    x, z, core, y = stn // 4, (stn // 2 % 2) * 2 + chan // 4, stn % 2, chan % 4
    along_x = [(x + step) % 4 * 32 for step in range(4)]
    along_y = [(y + step) % 4 for step in range(4)]

    def plane_of(outer):
        other_z = (z + outer + 1) % 4
        return other_z // 2 * 16 + other_z % 2 * 4 + (core + outer // 4) % 2 * 8

    def each_partner(act):
        @pl.loop(0, 8)
        def _(outer):
            base = plane_of(outer)
            for step_y in range(4):
                for step_x in range(4):
                    index = base + along_x[step_x] + along_y[step_y]
                    if step_x == 0 and step_y == 0:
                        pl.when(outer != 3)(functools.partial(act, index))
                    else:
                        act(index)

    table_copy = pltpu.make_async_copy(table_hbm, table, load_sem.at[parts])
    loads = []
    for part in range(parts):
        span = pl.ds(part * share, share)
        loads.append(pltpu.make_async_copy(volt_hbm.at[span], volt.at[span], load_sem.at[part]))
        loads[-1].start()
    small_copies = [
        pltpu.make_async_copy(taps_hbm, taps_ref, load_sem.at[parts + 1]),
        pltpu.make_async_copy(flags_hbm, flags_ref, load_sem.at[parts + 2]),
    ]
    for copy in small_copies:
        copy.start()
    table_copy.start()

    barrier = pltpu.get_barrier_semaphore()

    def greet(index):
        pl.semaphore_signal(barrier, inc=1, device_id=owner(index), device_id_type=MESH)

    each_partner(greet)

    for copy in loads + small_copies:
        copy.wait()

    def widened(feed, start, rows):
        flag = flags_ref[feed // 2].astype(jnp.float32)
        for tile in range(8):
            block = volt[feed, start : start + rows, tile * LANES : (tile + 1) * LANES].astype(jnp.float32)
            raw[tile, pl.ds(pl.multiple_of(feed * pitch + 8 + start, 8), rows), :] = block * flag

    @pl.loop(0, feeds)
    def _(feed):
        widened(feed, steps - 16, 16)

    for tile in range(8):
        for back in range(TAPS - 1):
            rows = raw[tile, pl.ds(8 + steps - (TAPS - 1) + back, feeds, stride=pitch), :]
            halo_src[pl.ds(back * feeds, feeds), pl.ds(tile * LANES, LANES)] = rows.astype(jnp.bfloat16)

    mixed_of = (mixed_even, mixed_odd)

    def filtered(half, both, odd):
        first = 4 - 4 * half
        for feed_of in range(4):
            feed = 4 * both + feed_of
            if half == 0:
                widened(feed, 0, steps - 16)
            for tile in range(8):
                weights = [
                    taps_ref[pl.ds(tap, 1), pl.ds((tile % 4) * LANES, LANES)] for tap in range(TAPS)
                ]
                rows = [
                    raw[tile, pl.ds(feed * pitch + 8 + first - 3 + shift, 8, stride=8), :]
                    for shift in range(7)
                ]
                sums = []
                for index in range(4):
                    total = weights[0] * rows[index]
                    for tap in range(1, TAPS):
                        total = total + weights[tap] * rows[index + tap]
                    sums.append(total)
                block = jnp.concatenate(sums, axis=0).astype(jnp.bfloat16)
                base = both // 2 * 2 * LANES + feed_of // 2 * LANES + feed_of % 2 * 32
                mixed_of[odd][
                    half, pl.ds(pl.multiple_of(base, 32), 32), tile * LANES : (tile + 1) * LANES
                ] = block
                other = (tile + 4) % 8
                turned = block if tile >= 4 else -block
                mixed_of[odd][
                    half, pl.ds(pl.multiple_of(base + 64, 32), 32), other * LANES : (other + 1) * LANES
                ] = turned

    depth = 2 * stations

    def transformed(half, pair, both, odd):
        rows = mixed_of[odd][half, pl.ds(pl.multiple_of(both // 2 * 256, 256), 256), :]
        out = lax.dot_general(
            table[pair * 2 * count : (pair + 1) * 2 * count, :], rows,
            (((1,), (1,)), ((), ())), preferred_element_type=jnp.float32,
        )
        planes[pl.ds(2 * both, 2 * count, stride=stations), :] = out[:, :LANES]
        planes[pl.ds(2 * both + 1, 2 * count, stride=stations), :] = out[:, LANES:]

    def packed(index):
        rows = planes[pl.ds(pl.multiple_of(index * depth, depth), depth), :]
        return rows.astype(jnp.bfloat16)

    halo = []
    has_next, has_last = chan < chan_count - 1, chan > 0

    def open_links():
        pl.semaphore_wait(barrier, count - 1)

        for back in range(TAPS - 1):
            span = pl.ds(back * feeds, feeds)
            halo.append(
                pltpu.make_async_remote_copy(
                    src_ref=halo_src.at[span], dst_ref=halo_dst.at[span],
                    send_sem=halo_send.at[back], recv_sem=halo_recv.at[back],
                    device_id=(stn, (chan + 1) % chan_count), device_id_type=MESH,
                )
            )
            pl.when(has_next)(halo[-1].start)

    def first_spectra(half):
        last = stations // 2 - 1
        filtered(half, 0, 0)

        def advance(step):
            for odd in range(2):
                transformed(half, 0, 2 * step + odd, odd)
                filtered(half, 2 * step + odd + 1, 1 - odd)

        ahead = 1 if half == 0 else 0
        pl.loop(0, ahead)(advance)
        if half == 0:
            open_links()
        pl.loop(ahead, last // 2)(advance)
        transformed(half, 0, last - 1, 0)
        filtered(half, last, 1)
        transformed(half, 0, last, 1)

    def second_spectra(half):
        @pl.loop(0, stations // 4)
        def _(step):
            for odd in range(2):
                transformed(half, 1, 2 * step + odd, odd)

    def send_spectra(half, pair):
        slot = 2 * pair + half

        @each_partner
        def _(index):
            a_src[slot, index] = packed(index)
            pltpu.make_async_remote_copy(
                src_ref=a_src.at[slot, index], dst_ref=a_dst.at[slot, me],
                send_sem=a_send.at[slot], recv_sem=a_recv.at[slot],
                device_id=owner(index), device_id_type=MESH,
            ).start()

        a_dst[slot, me] = packed(me)

    def all_spectra(half, pair):
        slot = 2 * pair + half
        ref = a_dst.at[slot, pl.ds(0, count - 1)]
        return pltpu.make_async_remote_copy(
            src_ref=ref, dst_ref=ref, send_sem=a_send.at[slot], recv_sem=a_recv.at[slot],
            device_id=owner(me), device_id_type=MESH,
        )

    table_copy.wait()
    first_spectra(0)
    send_spectra(0, 0)

    @pl.when(has_last)
    def _():
        for copy in halo:
            copy.wait_recv()
        for tile in range(8):
            for back in range(TAPS - 1):
                rows = halo_dst[pl.ds(back * feeds, feeds), pl.ds(tile * LANES, LANES)]
                raw[tile, pl.ds(8 - (TAPS - 1) + back, feeds, stride=pitch), :] = rows.astype(jnp.float32)

    @pl.when(jnp.logical_not(has_last))
    def _():
        for tile in range(8):
            for back in range(TAPS - 1):
                raw[tile, pl.ds(8 - (TAPS - 1) + back, feeds, stride=pitch), :] = jnp.zeros(
                    (feeds, LANES), jnp.float32
                )

    first_spectra(1)
    send_spectra(1, 0)
    second_spectra(0)
    send_spectra(0, 1)
    second_spectra(1)
    send_spectra(1, 1)

    lane = lax.broadcasted_iota(jnp.int32, (1, LANES), 1)
    first_part = lane % 64 < 32
    turn_sign = jnp.where(lane < 64, 1.0, -1.0)
    rows_total = stn_count * stations
    targets = [(stn + step) % stn_count for step in range(1, stn_count)]

    def correlated(own):
        for half in range(2):
            @pl.loop(0, chan_count // 2)
            def _(couple):
                first, second = (
                    jnp.concatenate(
                        [
                            a_dst[
                                2 * (own // 2) + half, block * chan_count + 2 * couple + source,
                                own % 2 * stations : (own % 2 + 1) * stations, :,
                            ]
                            for block in range(stn_count)
                        ],
                        axis=0,
                    ).astype(jnp.float32)
                    for source in range(2)
                )
                polars = [
                    jnp.where(first_part, first, pltpu.roll(second, 32, 1)),
                    jnp.where(first_part, pltpu.roll(first, 96, 1), second),
                ]
                lanes = pl.ds(pl.multiple_of((half * (chan_count // 2) + couple) * LANES, LANES), LANES)
                for polar, value in enumerate(polars):
                    turned = pltpu.roll(value, 64, 1) * turn_sign
                    terms[polar * rows_total : (polar + 1) * rows_total, lanes] = value.astype(jnp.bfloat16)
                    terms[(2 + polar) * rows_total : (3 + polar) * rows_total, lanes] = turned.astype(jnp.bfloat16)

        for part in range(2):
            out = lax.dot_general(
                terms[part * 2 * rows_total : (part + 1) * 2 * rows_total, :], terms[: 2 * rows_total, :],
                (((1,), (1,)), ((), ())), preferred_element_type=jnp.float32,
            )
            xx, xy = out[:rows_total, :rows_total], out[:rows_total, rows_total:]
            yx, yy = out[rows_total:, :rows_total], out[rows_total:, rows_total:]
            stokes = [
                (part, xx + yy), (2 + part, xx - yy), (4 + part, xy + yx),
                (7, yx - xy) if part == 0 else (6, xy - yx),
            ]
            for index, value in stokes:
                b_src[own, :, index] = value.astype(jnp.bfloat16).reshape(stn_count, stations, rows_total)
            for index, _ in stokes:
                for target in targets:
                    pltpu.make_async_remote_copy(
                        src_ref=b_src.at[own, target, index],
                        dst_ref=out_ref.at[stn * per_device + own, index],
                        send_sem=b_send, recv_sem=b_recv, device_id=(target, chan), device_id_type=MESH,
                    ).start()

    own_copies = []
    for own in range(per_device):
        if own % 2 == 0:
            all_spectra(0, own // 2).wait_recv()
            all_spectra(1, own // 2).wait_recv()
        correlated(own)

        own_copies.append(
            pltpu.make_async_copy(b_src.at[own, stn], out_ref.at[stn * per_device + own], own_sem.at[own])
        )
        own_copies[-1].start()

    for copy in halo:
        pl.when(has_next)(copy.wait_send)
    for pair in range(per_device // 2):
        for half in range(2):
            all_spectra(half, pair).wait_send()
    for copy in own_copies:
        copy.wait()
    ref = out_ref.at[pl.ds(0, (stn_count - 1) * per_device)]
    pltpu.make_async_remote_copy(
        src_ref=ref, dst_ref=ref, send_sem=b_send, recv_sem=b_recv,
        device_id=owner(me), device_id_type=MESH,
    ).wait()


def widen(scale, narrow, wide_hbm, wide, out_sem):
    parts = out_sem.shape[0]
    share = narrow.shape[0] // parts
    stores = []
    for part in range(parts):
        @pl.loop(part * share, (part + 1) * share)
        def _(row):
            wide[row] = narrow[row].astype(jnp.float32) * scale

        span = pl.ds(part * share, share)
        stores.append(pltpu.make_async_copy(wide.at[span], wide_hbm.at[span], out_sem.at[part]))
        stores[-1].start()
    for store in stores:
        store.wait()


def on_device(voltages, taps, flags):
    stn_count, chan_count = lax.axis_size("stn"), lax.axis_size("chan")
    count = stn_count * chan_count
    stations, polars, steps, width = voltages.shape
    feeds = stations * polars
    per_device = CHANNELS // count
    total = stn_count * stations
    vmem = pltpu.VMEM
    out_dims = (CHANNELS // chan_count, 8, stations, total)
    narrow = pl.pallas_call(
        kernel,
        out_shape=vmem(out_dims, jnp.bfloat16),
        in_specs=[
            pl.BlockSpec(memory_space=pltpu.HBM),
            pl.BlockSpec(memory_space=pltpu.HBM),
            pl.BlockSpec(memory_space=pltpu.HBM),
            pl.BlockSpec(memory_space=pltpu.HBM),
        ],
        out_specs=pl.BlockSpec(memory_space=vmem),
        scratch_shapes=[
            vmem(taps.shape, jnp.float32),
            pltpu.SMEM(flags.shape, jnp.int32),
            vmem((feeds, steps, width), jnp.bfloat16),
            vmem((CHANNELS, width), jnp.bfloat16),
            vmem((8, feeds * (steps + 8), LANES), jnp.float32),
            vmem((2, stations // 2 * LANES, width), jnp.bfloat16),
            vmem((2, stations // 2 * LANES, width), jnp.bfloat16),
            vmem((2 * count * stations, LANES), jnp.float32),
            vmem((per_device, count, 2 * stations, LANES), jnp.bfloat16),
            vmem((per_device, count, 2 * stations, LANES), jnp.bfloat16),
            vmem((4 * total, chan_count * LANES), jnp.bfloat16),
            vmem((per_device, stn_count, 8, stations, total), jnp.bfloat16),
            vmem(((TAPS - 1) * feeds, width), jnp.bfloat16),
            vmem(((TAPS - 1) * feeds, width), jnp.bfloat16),
            pltpu.SemaphoreType.DMA((7,)),
            pltpu.SemaphoreType.DMA((TAPS - 1,)),
            pltpu.SemaphoreType.DMA((TAPS - 1,)),
            pltpu.SemaphoreType.DMA((per_device,)),
            pltpu.SemaphoreType.DMA((per_device,)),
            pltpu.SemaphoreType.DMA,
            pltpu.SemaphoreType.DMA,
            pltpu.SemaphoreType.DMA((per_device,)),
        ],
        compiler_params=pltpu.CompilerParams(
            collective_id=0, has_side_effects=True, vmem_limit_bytes=50 * 1024 * 1024
        ),
        name="correlate",
    )(voltages.reshape(feeds, steps, width), taps, flags, half_table(stn_count, chan_count))
    return pl.pallas_call(
        functools.partial(widen, 1.0 / (steps * chan_count)),
        out_shape=jax.ShapeDtypeStruct(out_dims, jnp.float32),
        in_specs=[pl.BlockSpec(memory_space=vmem)],
        out_specs=pl.BlockSpec(memory_space=pl.ANY),
        scratch_shapes=[
            vmem(out_dims, jnp.float32),
            pltpu.SemaphoreType.DMA((16,)),
        ],
        compiler_params=pltpu.CompilerParams(vmem_limit_bytes=16 * 1024 * 1024),
        name="widen",
    )(narrow)


def solution(mesh):
    return jax.shard_map(
        on_device,
        mesh=mesh,
        in_specs=(P("stn", None, "chan", None), P(), P("stn")),
        out_specs=P("chan", None, "stn", None),
        check_vma=False,
    )
```
